32 devices in a mesh: grp: 4 (over x, core), seq: 8 (over z, y).
Axes of the slice: x: 2, y: 2, z: 4, core: 2. Of those that a mesh axis runs over, the one named last changes fastest.
Arguments:
- queries: bfloat16 [1, 4096, 2048], P(None, ('grp', 'seq')), may hold values from -6 to 6
- key_vectors: bfloat16 [1, 4096, 2048], P(None, ('grp', 'seq')), may hold values from -6 to 6
- values: bfloat16 [1, 4096, 2048], P(None, ('grp', 'seq')), may hold values from -6 to 6
- log_decay: bfloat16 [1, 4096, 2048], P(None, ('grp', 'seq')), may hold values from -0.8 to 0, as said below
- write_rate: float32 [1, 16, 4096], P(None, None, ('grp', 'seq')), may hold values from 0 to 1, as said below
- out_gate: bfloat16 [1, 4096, 2048], P(None, ('grp', 'seq')), may hold values from -6 to 6
Outputs:
- layer_output: bfloat16 [1, 4096, 2048], P(None, ('grp', 'seq'))
The draws below stay inside these ranges and needn't reach their ends.
Inputs may be any that keep to these rules, and one draw needn't show every extreme that they name: log_decay is negative. write_rate is positive.
All inputs are finite; a program needn't handle non-finite values.
Results may differ from the reference program's by a relative error of at most 0.001.
Values sent between devices are 32-bit elements; how exact they have to be, the bound alone decides.
A program may use at most 128 MiB of HBM per device.

```python
import math
import jax
import jax.numpy as jnp
from jax import lax

LOCAL_HEADS = 16
DK = 128
BLOCK = 64
SEQUENCE_COUNT = 1
TOK_DEV = 128
SEQUENCE_LENGTH = 4096


def slow_heads(key):
    kind_key = jax.random.fold_in(key, 11)
    slow_share = 0.5
    return jax.random.uniform(kind_key, (SEQUENCE_COUNT, LOCAL_HEADS)) < slow_share


def draw_log_decay(key, part):
    picked_heads = slow_heads(key)
    random_subkeys = jax.random.split(jax.random.fold_in(key, 23), 5)
    channel_key = jax.random.fold_in(key, 29)
    gentle_channels = jax.random.uniform(channel_key, (SEQUENCE_COUNT, 1, LOCAL_HEADS, DK)) < 0.25
    segments = SEQUENCE_LENGTH // TOK_DEV
    segment = jnp.exp(jax.random.uniform(random_subkeys[0], (SEQUENCE_COUNT, segments, 1, 1), minval=-math.log(2.0), maxval=math.log(2.0)))
    segment = jnp.repeat(segment, TOK_DEV, axis=1)
    gentle = jnp.exp(jax.random.uniform(random_subkeys[1], (SEQUENCE_COUNT, SEQUENCE_LENGTH, LOCAL_HEADS, DK), minval=math.log(0.05), maxval=math.log(0.5))) / SEQUENCE_LENGTH
    strong = jnp.exp(jax.random.uniform(random_subkeys[2], (SEQUENCE_COUNT, SEQUENCE_LENGTH, LOCAL_HEADS, DK), minval=math.log(1.0 / 50.0), maxval=math.log(1.0 / 30.0)))
    use_gentle = jnp.logical_or(picked_heads[:, None, :, None], gentle_channels)
    rate_values = jnp.where(use_gentle, gentle, strong) * segment
    token_positions = jax.random.randint(random_subkeys[3], (SEQUENCE_COUNT, 3), 0, SEQUENCE_LENGTH)
    spike_locations = jnp.arange(SEQUENCE_LENGTH, dtype=jnp.int32)
    spike_selected = jnp.any(spike_locations[None, :, None] == token_positions[:, None, :], axis=-1)
    spike_lowering = jax.random.uniform(random_subkeys[4], (SEQUENCE_COUNT, SEQUENCE_LENGTH, LOCAL_HEADS, 1), minval=math.log(0.5), maxval=math.log(0.8))
    applied_rates = jnp.logical_and(spike_selected[:, :, None, None], picked_heads[:, None, :, None])
    final_output = -rate_values + jnp.where(applied_rates, spike_lowering, 0.0)
    return final_output.reshape(SEQUENCE_COUNT, SEQUENCE_LENGTH, LOCAL_HEADS * DK).astype(jnp.bfloat16)


def draw_write_rate(key, part):
    picked_heads = slow_heads(key)
    random_subkeys = jax.random.split(jax.random.fold_in(key, 31), 2)
    gentle = jax.random.uniform(random_subkeys[0], (SEQUENCE_COUNT, LOCAL_HEADS, SEQUENCE_LENGTH), minval=0.3, maxval=1.0) * DK / SEQUENCE_LENGTH
    strong = jax.random.uniform(random_subkeys[1], (SEQUENCE_COUNT, LOCAL_HEADS, SEQUENCE_LENGTH), minval=0.1, maxval=1.0)
    return jnp.where(picked_heads[:, :, None], gentle, strong).astype(jnp.float32)


def shard_levels(key, shape, cuts, least, top_value):
    factor_of, own = 1.0, jax.random.fold_in(key, 6)
    for dim, shards_of in cuts:
        draws = jnp.exp(jax.random.uniform(jax.random.fold_in(own, dim), (shards_of,), jnp.float32, least / len(cuts), top_value / len(cuts)))
        factor_of = factor_of * jnp.repeat(draws, shape[dim] // shards_of).reshape([-1 if axis == dim else 1 for axis in range(len(shape))])
    return factor_of


def bell_draw(rng, shape, spread, limit, cuts=(), held_as=jnp.bfloat16):
    values = spread * jax.random.normal(rng, shape, jnp.float32)
    if cuts:
        values = values * shard_levels(rng, shape, cuts, -0.22, 0.18)
    return jnp.clip(values, -limit, limit).astype(held_as)


def setup_inputs(seed: int = 0) -> dict:
    key_of = jax.random.split(jax.random.key(seed), 7)
    queries = bell_draw(key_of[0], (SEQUENCE_COUNT, SEQUENCE_LENGTH, LOCAL_HEADS * DK), 1.0, 6.0, ((1, 32),))
    key_vectors = bell_draw(key_of[1], (SEQUENCE_COUNT, SEQUENCE_LENGTH, LOCAL_HEADS * DK), 1.0, 6.0, ((1, 32),))
    values = bell_draw(key_of[2], (SEQUENCE_COUNT, SEQUENCE_LENGTH, LOCAL_HEADS * DK), 1.0, 6.0, ((1, 32),))
    log_decay = draw_log_decay(jax.random.fold_in(key_of[6], 71), 0)
    write_rate = draw_write_rate(jax.random.fold_in(key_of[6], 71), 0)
    out_gate = bell_draw(key_of[5], (SEQUENCE_COUNT, SEQUENCE_LENGTH, LOCAL_HEADS * DK), 1.5, 6.0, ((1, 32),))
    return dict(queries=queries, key_vectors=key_vectors, values=values, log_decay=log_decay, write_rate=write_rate, out_gate=out_gate)


precise_mode = lax.Precision.HIGHEST

def matmul(left, right):
    return jnp.einsum('...ij,...jk->...ik', left, right, precision=precise_mode)

def inner_rows(left, right):
    return jnp.einsum('...ci,...cj->...ij', left, right, precision=precise_mode)

def outer_rows(left, right):
    return jnp.einsum('...tc,...sc->...ts', left, right, precision=precise_mode)

def unit_lower_inverse(lower_part):
    extent = lower_part.shape[-1]
    identity = jnp.eye(extent, dtype=lower_part.dtype)
    powered = lower_part
    inverse = identity - lower_part
    for squaring in range(extent.bit_length() - 2):
        powered = matmul(powered, powered)
        inverse = matmul(inverse, identity + powered)
    return inverse

def block_terms(query_f, key_unit, decay_log, rate_block):
    extent = query_f.shape[-2]
    cumulative = jnp.cumsum(decay_log, axis=-2)
    growing = jnp.exp(cumulative)
    shrinking = jnp.exp(-cumulative)
    to_end = jnp.exp(cumulative[..., -1:, :] - cumulative)
    key_grow = key_unit * growing
    key_shrink = key_unit * shrinking
    query_grow = query_f * growing
    key_end = key_unit * to_end * rate_block[..., None]
    row_ids = lax.broadcasted_iota(jnp.int32, (extent, extent), 0)
    col_ids = lax.broadcasted_iota(jnp.int32, (extent, extent), 1)
    affinity = outer_rows(key_grow, key_shrink) * rate_block[..., None, :]
    lower_part = jnp.where(row_ids > col_ids, affinity, 0.0)
    attend = jnp.where(row_ids >= col_ids, outer_rows(query_grow, key_shrink) * rate_block[..., None, :], 0.0)
    inverse = unit_lower_inverse(lower_part)
    decay_end = jnp.exp(cumulative[..., -1, :])
    return (query_grow, key_grow, key_end, attend, inverse, decay_end)

def reference(queries, key_vectors, values, log_decay, write_rate, out_gate):
    seq_count, seq_len, features = queries.shape
    blocks = seq_len // BLOCK

    def to_blocks(tensor):
        shaped = tensor.reshape(seq_count, blocks, BLOCK, LOCAL_HEADS, DK)
        return jnp.transpose(shaped, (1, 0, 3, 2, 4))
    rate_blocks = jnp.transpose(write_rate.reshape(seq_count, LOCAL_HEADS, blocks, BLOCK), (2, 0, 1, 3))

    def advance(memory, inputs):
        query_in, key_in, value_in, decay_in, rate_in, gate_in = inputs
        query_f = query_in.astype(jnp.float32)
        key_f = key_in.astype(jnp.float32)
        key_unit = key_f / jnp.sqrt(lax.optimization_barrier(jnp.sum(key_f * key_f, axis=-1, keepdims=True)) + 1e-06)
        query_grow, key_grow, key_end, attend, inverse, decay_end = block_terms(query_f, key_unit, decay_in.astype(jnp.float32), rate_in)
        fresh_vals = matmul(inverse, value_in.astype(jnp.float32) - matmul(key_grow, memory))
        raw_out = matmul(query_grow, memory) + matmul(attend, fresh_vals)
        memory = decay_end[..., :, None] * memory + inner_rows(key_end, fresh_vals)
        scaled = raw_out / jnp.sqrt(lax.optimization_barrier(jnp.mean(raw_out * raw_out, axis=-1, keepdims=True)) + 1e-05)
        final_output = (scaled * jax.nn.sigmoid(gate_in.astype(jnp.float32))).astype(jnp.bfloat16)
        return (memory, final_output)
    initial = jnp.zeros((seq_count, LOCAL_HEADS, DK, DK), jnp.float32)
    _, results = lax.scan(advance, initial, (to_blocks(queries), to_blocks(key_vectors), to_blocks(values), to_blocks(log_decay), rate_blocks, to_blocks(out_gate)))
    return jnp.transpose(results, (1, 0, 3, 2, 4)).reshape(seq_count, seq_len, features)
```

```python
import functools
import jax
import jax.numpy as jnp
from jax import lax
from jax.experimental import pallas as pl
from jax.experimental.pallas import tpu as pltpu
from jax.sharding import PartitionSpec as P

BLOCK = 64
BATCH = 4
MESH = pl.DeviceIdType.MESH
F32 = jnp.float32
BF16 = jnp.bfloat16


def split(value):
    high = value.astype(BF16)
    return high, (value - high.astype(F32)).astype(BF16)


def mul(left, right):
    width = right.shape[1]
    lhs = jnp.concatenate(split(left), axis=1)
    parts = jnp.concatenate(split(right), axis=1)
    out = jnp.dot(lhs, jnp.concatenate([parts, parts], axis=0), preferred_element_type=F32)
    return out[:, :width] + out[:, width:]


def mul_rows(left, right):
    width = right.shape[0]
    lhs = jnp.concatenate(split(left), axis=1)
    parts = jnp.concatenate(split(right), axis=0)
    rhs = jnp.concatenate([parts, parts], axis=1)
    out = lax.dot_general(lhs, rhs, (((1,), (1,)), ((), ())), preferred_element_type=F32)
    return out[:, :width] + out[:, width:]


def mul_wide(left, right):
    high, low = split(left)
    r_high, r_low = split(right)
    lhs = jnp.concatenate([high, low], axis=1)
    rhs = jnp.concatenate([r_high, r_high], axis=0)
    return jnp.dot(lhs, rhs, preferred_element_type=F32) + jnp.dot(
        high, r_low, preferred_element_type=F32
    )


def local_terms(queries, keys, values, decays, rates):
    extent, size = queries[0].shape
    half = extent // 2
    rows = lax.broadcasted_iota(jnp.int32, (extent, extent), 0)
    cols = lax.broadcasted_iota(jnp.int32, (extent, extent), 1)
    same = (rows >= half) == (cols >= half)
    eye = jnp.where(rows == cols, 1.0, 0.0).astype(F32)
    ones = jnp.where(rows >= cols, 1.0, 0.0).astype(BF16)
    cums = [jnp.dot(ones, decay, preferred_element_type=F32) for decay in decays]
    q_f = [query.astype(F32) for query in queries]
    units = []
    for key in keys:
        key_f = key.astype(F32)
        units.append(key_f * lax.rsqrt(jnp.sum(key_f * key_f, axis=-1, keepdims=True) + 1e-06))
    pairs = []
    for query, unit, cum in zip(q_f, units, cums):
        middle = cum[half - 1 : half]
        grow = jnp.exp(cum - middle)
        pairs.append(
            mul_rows(
                jnp.concatenate([unit * grow, query * grow], axis=0), unit * jnp.exp(middle - cum)
            )
        )
    lowers, attends = [], []
    for pair, rate in zip(pairs, rates):
        lowers.append(jnp.where(rows > cols, pair[:extent] * rate, 0.0))
        attends.append(jnp.where(rows >= cols, pair[extent:] * rate, 0.0))
    diag = [jnp.where(same, lower, 0.0) for lower in lowers]
    below = [jnp.where(same, 0.0, lower) for lower in lowers]
    inverse = [eye - part for part in diag]
    power = [mul(part, part) for part in diag]
    for _ in range(half.bit_length() - 3):
        both = [mul(jnp.concatenate([x, p], axis=0), p) for x, p in zip(inverse, power)]
        inverse = [x + b[:extent] for x, b in zip(inverse, both)]
        power = [b[extent:] for b in both]
    inverse = [x + mul(x, p) for x, p in zip(inverse, power)]
    corner = [mul(x[half:], c) for x, c in zip(inverse, below)]
    corner = [mul(c, x) for c, x in zip(corner, inverse)]
    inverse = [
        jnp.concatenate([x[:half], x[half:] - c], axis=0) for x, c in zip(inverse, corner)
    ]
    from_start = [jnp.exp(cum) for cum in cums]
    carry = [
        mul_wide(x, jnp.concatenate([unit * grow, value.astype(F32)], axis=1))
        for x, unit, grow, value in zip(inverse, units, from_start, values)
    ]
    results = []
    for query, unit, cum, grow, attend, rate, carried in zip(
        q_f, units, cums, from_start, attends, rates, carry
    ):
        last = cum[extent - 1 : extent]
        key_end = jnp.transpose(unit * jnp.exp(last - cum)) * rate
        out = mul_wide(jnp.concatenate([attend, key_end], axis=0), carried)
        step_map = jnp.where(rows == cols, jnp.exp(last), 0.0) - out[extent:, :size]
        results.append(
            (
                query * grow - out[:extent, :size],
                out[:extent, size:],
                jnp.concatenate([step_map, out[extent:, size:]], axis=1),
            )
        )
    return results


def kernel(
    groups, count, heads,
    q_ref, k_ref, v_ref, d_ref, r_ref, g_ref, o_ref,
    sent, arrived, prior, entry, onward, starts, begin, reach, local,
    up_send, up_recv, chain_send, chain_recv, down_send, down_recv,
):
    grp, me = lax.axis_index("grp"), lax.axis_index("seq")
    per = max(heads // count, 1)
    owners = heads // per
    extent = q_ref.shape[0]
    size = q_ref.shape[1] // heads
    everyone = owners == count

    def when_owner(body):
        if everyone:
            body()
        else:
            pl.when(me < owners)(body)

    barrier = pltpu.get_barrier_semaphore()

    def greet(step, _):
        peer = lax.rem(me + step, count)
        pl.semaphore_signal(barrier, inc=1, device_id=(grp, peer), device_id_type=MESH)
        return 0

    lax.fori_loop(1, count, greet, 0)

    @pl.when(grp > 0)
    def _():
        pl.semaphore_signal(barrier, inc=1, device_id=(grp - 1, me), device_id_type=MESH)

    @pl.when(grp < groups - 1)
    def _():
        pl.semaphore_signal(barrier, inc=1, device_id=(grp + 1, me), device_id_type=MESH)

    beside = jnp.minimum(grp, 1) + jnp.minimum(groups - 1 - grp, 1)
    pl.semaphore_wait(barrier, count - 1 + beside)

    def columns(head):
        return pl.ds(pl.multiple_of(head * size, size), size)

    def up_copy(head, shard, owner):
        return pltpu.make_async_remote_copy(
            src_ref=sent.at[head],
            dst_ref=arrived.at[shard, lax.rem(head, per)],
            send_sem=up_send.at[head],
            recv_sem=up_recv.at[shard, lax.rem(head, per)],
            device_id=(grp, owner),
            device_id_type=MESH,
        )

    def compute(step, _):
        picked = [
            lax.rem(step * BATCH + index + per * (me + 1), heads) for index in range(BATCH)
        ]
        spans = [columns(head) for head in picked]
        results = local_terms(
            [q_ref[:, span] for span in spans],
            [k_ref[:, span] for span in spans],
            [v_ref[:, span] for span in spans],
            [d_ref[:, span] for span in spans],
            [r_ref[pl.ds(head, 1), :] for head in picked],
        )
        for head, (head_reach, head_local, head_step) in zip(picked, results):
            reach[head] = head_reach
            local[head] = head_local
            sent[head] = head_step
            owner = lax.div(head, per)

            @pl.when(owner != me)
            def _():
                up_copy(head, me, owner).start()

            @pl.when(owner == me)
            def _():
                arrived[me, lax.rem(head, per)] = head_step

        return 0

    lax.fori_loop(0, heads // BATCH, compute, 0)

    rows = lax.broadcasted_iota(jnp.int32, (size, 2 * size), 0)
    cols = lax.broadcasted_iota(jnp.int32, (size, 2 * size), 1)

    def compose():
        for index in range(per):
            prior[0, index] = jnp.where(rows == cols, 1.0, 0.0).astype(F32)

        def advance(shard, _):
            @pl.when(shard != me)
            def _():
                for index in range(per):
                    up_copy(me * per + index, shard, me).wait_recv()

            for index in range(per):
                step = arrived[shard, index]
                product = mul_wide(step[:, :size], prior[shard, index])
                prior[shard + 1, index, :, :size] = product[:, :size]
                prior[shard + 1, index, :, size:] = product[:, size:] + step[:, size:]
            return 0

        lax.fori_loop(0, count, advance, 0)

        def chain_copy(target):
            return pltpu.make_async_remote_copy(
                src_ref=onward,
                dst_ref=entry,
                send_sem=chain_send,
                recv_sem=chain_recv,
                device_id=(target, me),
                device_id_type=MESH,
            )

        @pl.when(grp == 0)
        def _():
            entry[...] = jnp.zeros_like(entry)

        @pl.when(grp > 0)
        def _():
            chain_copy(grp).wait_recv()

        @pl.when(grp < groups - 1)
        def _():
            for index in range(per):
                total = prior[count, index]
                onward[index] = mul(total[:, :size], entry[index]) + total[:, size:]
            chain_copy(grp + 1).start()

        def give(step, _):
            shard = lax.rem(me + 1 + step, count)
            for index in range(per):
                before = prior[shard, index]
                starts[shard, index] = mul(before[:, :size], entry[index]) + before[:, size:]

            @pl.when(shard != me)
            def _():
                down_copy(shard, me).start()

            @pl.when(shard == me)
            def _():
                begin[pl.ds(me * per, per)] = starts[shard]

            return 0

        lax.fori_loop(0, count, give, 0)

        @pl.when(grp < groups - 1)
        def _():
            chain_copy(grp + 1).wait_send()

    def down_copy(shard, owner):
        return pltpu.make_async_remote_copy(
            src_ref=starts.at[shard],
            dst_ref=begin.at[pl.ds(owner * per, per)],
            send_sem=down_send.at[shard],
            recv_sem=down_recv.at[owner],
            device_id=(grp, shard),
            device_id_type=MESH,
        )

    when_owner(compose)

    def finish(step, _):
        owner = lax.rem(me + owners - step, owners) if everyone else step

        @pl.when(owner != me)
        def _():
            down_copy(me, owner).wait_recv()

        for index in range(per):
            head = owner * per + index
            raw = mul(reach[head], begin[head]) + local[head]
            scaled = raw * lax.rsqrt(jnp.mean(raw * raw, axis=-1, keepdims=True) + 1e-05)
            gate = g_ref[:, columns(head)].astype(F32)
            o_ref[:, columns(head)] = (scaled / (1.0 + jnp.exp(-gate))).astype(BF16)
        return 0

    lax.fori_loop(0, owners, finish, 0)

    def drain_up(head, _):
        owner = lax.div(head, per)

        @pl.when(owner != me)
        def _():
            up_copy(head, me, owner).wait_send()

        return 0

    lax.fori_loop(0, heads, drain_up, 0)

    def drain_down():
        def one(shard, _):
            @pl.when(shard != me)
            def _():
                down_copy(shard, me).wait_send()

            return 0

        lax.fori_loop(0, count, one, 0)

    when_owner(drain_down)


def shards(groups, count, queries, key_vectors, values, log_decay, write_rate, out_gate):
    seq_count, local_len, features = queries.shape
    heads = write_rate.shape[1]
    size = features // heads
    per = max(heads // count, 1)
    dma = pltpu.SemaphoreType.DMA
    square = (size, size)
    wide = (size, 2 * size)
    call = pl.pallas_call(
        functools.partial(kernel, groups, count, heads),
        out_shape=jax.ShapeDtypeStruct((local_len, features), BF16),
        in_specs=[pl.BlockSpec(memory_space=pltpu.VMEM)] * 6,
        out_specs=pl.BlockSpec(memory_space=pltpu.VMEM),
        scratch_shapes=[
            pltpu.VMEM((heads, *wide), F32),
            pltpu.VMEM((count, per, *wide), F32),
            pltpu.VMEM((count + 1, per, *wide), F32),
            pltpu.VMEM((per, *square), F32),
            pltpu.VMEM((per, *square), F32),
            pltpu.VMEM((count, per, *square), F32),
            pltpu.VMEM((heads, *square), F32),
            pltpu.VMEM((heads, local_len, size), F32),
            pltpu.VMEM((heads, local_len, size), F32),
            dma((heads,)),
            dma((count, per)),
            dma,
            dma,
            dma((count,)),
            dma((heads // per,)),
        ],
        compiler_params=pltpu.CompilerParams(
            collective_id=0, has_side_effects=True, vmem_limit_bytes=48 * 1024 * 1024
        ),
        name="delta_attention",
    )
    result = call(
        queries[0], key_vectors[0], values[0], log_decay[0], write_rate[0], out_gate[0]
    )
    return result[None]


def solution(mesh):
    spread = P(None, ("grp", "seq"), None)
    return jax.shard_map(
        functools.partial(shards, mesh.shape["grp"], mesh.shape["seq"]),
        mesh=mesh,
        in_specs=(spread, spread, spread, spread, P(None, None, ("grp", "seq")), spread),
        out_specs=spread,
        check_vma=False,
    )
```

```python
import functools
import jax
import jax.numpy as jnp
from jax import lax
from jax.experimental import pallas as pl
from jax.experimental.pallas import tpu as pltpu
from jax.sharding import PartitionSpec as P

BLOCK = 64
BATCH = 4
MESH = pl.DeviceIdType.MESH
F32 = jnp.float32
BF16 = jnp.bfloat16


def split(value):
    high = value.astype(BF16)
    return high, (value - high.astype(F32)).astype(BF16)


def mul(left, right):
    width = right.shape[1]
    lhs = jnp.concatenate(split(left), axis=1)
    parts = jnp.concatenate(split(right), axis=1)
    out = jnp.dot(lhs, jnp.concatenate([parts, parts], axis=0), preferred_element_type=F32)
    return out[:, :width] + out[:, width:]


def mul_rows(left, right):
    width = right.shape[0]
    lhs = jnp.concatenate(split(left), axis=1)
    parts = jnp.concatenate(split(right), axis=0)
    rhs = jnp.concatenate([parts, parts], axis=1)
    out = lax.dot_general(lhs, rhs, (((1,), (1,)), ((), ())), preferred_element_type=F32)
    return out[:, :width] + out[:, width:]


def mul_wide(left, right):
    high, low = split(left)
    r_high, r_low = split(right)
    lhs = jnp.concatenate([high, low], axis=1)
    rhs = jnp.concatenate([r_high, r_high], axis=0)
    return jnp.dot(lhs, rhs, preferred_element_type=F32) + jnp.dot(
        high, r_low, preferred_element_type=F32
    )


def local_terms(queries, keys, values, decays, rates):
    extent, size = queries[0].shape
    half = extent // 2
    rows = lax.broadcasted_iota(jnp.int32, (extent, extent), 0)
    cols = lax.broadcasted_iota(jnp.int32, (extent, extent), 1)
    same = (rows >= half) == (cols >= half)
    eye = jnp.where(rows == cols, 1.0, 0.0).astype(F32)
    ones = jnp.where(rows >= cols, 1.0, 0.0).astype(BF16)
    cums = [jnp.dot(ones, decay, preferred_element_type=F32) for decay in decays]
    q_f = [query.astype(F32) for query in queries]
    units = []
    for key in keys:
        key_f = key.astype(F32)
        units.append(key_f * lax.rsqrt(jnp.sum(key_f * key_f, axis=-1, keepdims=True) + 1e-06))
    pairs = []
    for query, unit, cum in zip(q_f, units, cums):
        middle = cum[half - 1 : half]
        grow = jnp.exp(cum - middle)
        pairs.append(
            mul_rows(
                jnp.concatenate([unit * grow, query * grow], axis=0), unit * jnp.exp(middle - cum)
            )
        )
    lowers, attends = [], []
    for pair, rate in zip(pairs, rates):
        lowers.append(jnp.where(rows > cols, pair[:extent] * rate, 0.0))
        attends.append(jnp.where(rows >= cols, pair[extent:] * rate, 0.0))
    diag = [jnp.where(same, lower, 0.0) for lower in lowers]
    below = [jnp.where(same, 0.0, lower) for lower in lowers]
    inverse = [eye - part for part in diag]
    power = [mul(part, part) for part in diag]
    for _ in range(half.bit_length() - 3):
        both = [mul(jnp.concatenate([x, p], axis=0), p) for x, p in zip(inverse, power)]
        inverse = [x + b[:extent] for x, b in zip(inverse, both)]
        power = [b[extent:] for b in both]
    inverse = [x + mul(x, p) for x, p in zip(inverse, power)]
    corner = [mul(x[half:], c) for x, c in zip(inverse, below)]
    corner = [mul(c, x) for c, x in zip(corner, inverse)]
    inverse = [
        jnp.concatenate([x[:half], x[half:] - c], axis=0) for x, c in zip(inverse, corner)
    ]
    from_start = [jnp.exp(cum) for cum in cums]
    carry = [
        mul_wide(x, jnp.concatenate([unit * grow, value.astype(F32)], axis=1))
        for x, unit, grow, value in zip(inverse, units, from_start, values)
    ]
    results = []
    for query, unit, cum, grow, attend, rate, carried in zip(
        q_f, units, cums, from_start, attends, rates, carry
    ):
        last = cum[extent - 1 : extent]
        key_end = jnp.transpose(unit * jnp.exp(last - cum)) * rate
        out = mul_wide(jnp.concatenate([attend, key_end], axis=0), carried)
        step_map = jnp.where(rows == cols, jnp.exp(last), 0.0) - out[extent:, :size]
        results.append(
            (
                query * grow - out[:extent, :size],
                out[:extent, size:],
                jnp.concatenate([step_map, out[extent:, size:]], axis=1),
            )
        )
    return results


def kernel(
    groups, count, heads,
    q_hbm, k_hbm, v_hbm, d_hbm, g_hbm, r_ref, o_hbm,
    q_ref, k_ref, v_ref, d_ref, g_ref, o_ref,
    sent, arrived, prior, total_in, pair_in, entry, onward, starts, begin, reach, local,
    load_sem, gate_sem, store_sem,
    up_send, up_recv, total_send, total_recv, pair_send, pair_recv, down_send, down_recv,
):
    grp, me = lax.axis_index("grp"), lax.axis_index("seq")
    per = max(heads // count, 1)
    owners = heads // per
    extent = q_ref.shape[0]
    size = q_ref.shape[1] // heads
    everyone = owners == count
    batches = heads // BATCH
    first_batch = lax.div(per * me, BATCH) + 1
    pair, odd = lax.div(grp, 2), lax.rem(grp, 2)
    last_pair = groups // 2 - 1

    def when_owner(body):
        if everyone:
            body()
        else:
            pl.when(me < owners)(body)

    def greet_at(group, seq):
        pl.semaphore_signal(barrier, inc=1, device_id=(group, seq), device_id_type=MESH)

    barrier = pltpu.get_barrier_semaphore()

    def greet(step, _):
        greet_at(grp, lax.rem(me + step, count))
        return 0

    lax.fori_loop(1, count, greet, 0)

    @pl.when(odd == 0)
    def _():
        greet_at(grp + 1, me)

    @pl.when(odd == 1)
    def _():
        greet_at(grp - 1, me)

    @pl.when(jnp.logical_and(odd == 0, pair > 0))
    def _():
        greet_at(grp - 1, me)

    @pl.when(jnp.logical_and(odd == 1, pair > 0))
    def _():
        greet_at(grp - 2, me)

    @pl.when(jnp.logical_and(odd == 1, pair < last_pair))
    def _():
        greet_at(grp + 1, me)
        greet_at(grp + 2, me)

    def batch_columns(step):
        batch = lax.rem(step + first_batch, batches)
        return batch, pl.ds(pl.multiple_of(batch * (BATCH * size), BATCH * size), BATCH * size)

    def load(step):
        batch, span = batch_columns(step)
        return [
            pltpu.make_async_copy(far.at[:, span], near.at[:, span], load_sem.at[index, batch])
            for index, (far, near) in enumerate(
                [(d_hbm, d_ref), (k_hbm, k_ref), (q_hbm, q_ref), (v_hbm, v_ref)]
            )
        ]

    for step in range(batches):
        for copy in load(step):
            copy.start()
    gate_copy = pltpu.make_async_copy(g_hbm, g_ref, gate_sem)
    gate_copy.start()

    beside = 1 + jnp.minimum(pair, 1) + 2 * odd * jnp.minimum(last_pair - pair, 1)
    pl.semaphore_wait(barrier, count - 1 + beside)

    def columns(head):
        return pl.ds(pl.multiple_of(head * size, size), size)

    def up_copy(head, shard, owner):
        return pltpu.make_async_remote_copy(
            src_ref=sent.at[head],
            dst_ref=arrived.at[shard, lax.rem(head, per)],
            send_sem=up_send.at[head],
            recv_sem=up_recv.at[shard, lax.rem(head, per)],
            device_id=(grp, owner),
            device_id_type=MESH,
        )

    def compute(step, _):
        for copy in load(step):
            copy.wait()
        batch, _unused = batch_columns(step)
        picked = [batch * BATCH + index for index in range(BATCH)]
        spans = [columns(head) for head in picked]
        results = local_terms(
            [q_ref[:, span] for span in spans],
            [k_ref[:, span] for span in spans],
            [v_ref[:, span] for span in spans],
            [d_ref[:, span] for span in spans],
            [r_ref[pl.ds(head, 1), :] for head in picked],
        )
        for head, (head_reach, head_local, head_step) in zip(picked, results):
            reach[head] = head_reach
            local[head] = head_local
            sent[head] = head_step
            owner = lax.div(head, per)

            @pl.when(owner != me)
            def _():
                up_copy(head, me, owner).start()

            @pl.when(owner == me)
            def _():
                arrived[me, lax.rem(head, per)] = head_step

        return 0

    lax.fori_loop(0, batches, compute, 0)

    rows = lax.broadcasted_iota(jnp.int32, (size, 2 * size), 0)
    cols = lax.broadcasted_iota(jnp.int32, (size, 2 * size), 1)

    def join(late, early):
        product = mul_wide(late[:, :size], early)
        return product[:, :size], product[:, size:] + late[:, size:]

    def apply(step, state):
        return mul(step[:, :size], state) + step[:, size:]

    def total_copy(target):
        return pltpu.make_async_remote_copy(
            src_ref=prior.at[count],
            dst_ref=total_in,
            send_sem=total_send,
            recv_sem=total_recv,
            device_id=(target, me),
            device_id_type=MESH,
        )

    def pair_copy(ahead):
        return pltpu.make_async_remote_copy(
            src_ref=onward,
            dst_ref=pair_in,
            send_sem=pair_send.at[ahead - 1],
            recv_sem=pair_recv,
            device_id=(grp + ahead, me),
            device_id_type=MESH,
        )

    def down_copy(shard, owner):
        return pltpu.make_async_remote_copy(
            src_ref=starts.at[shard],
            dst_ref=begin.at[pl.ds(owner * per, per)],
            send_sem=down_send.at[shard],
            recv_sem=down_recv.at[owner],
            device_id=(grp, shard),
            device_id_type=MESH,
        )

    def compose():
        for index in range(per):
            prior[0, index] = jnp.where(rows == cols, 1.0, 0.0).astype(F32)

        def advance(shard, _):
            @pl.when(shard != me)
            def _():
                for index in range(per):
                    up_copy(me * per + index, shard, me).wait_recv()

            for index in range(per):
                whole, added = join(arrived[shard, index], prior[shard, index])
                prior[shard + 1, index, :, :size] = whole
                prior[shard + 1, index, :, size:] = added
            return 0

        lax.fori_loop(0, count, advance, 0)

        @pl.when(odd == 0)
        def _():
            total_copy(grp + 1).start()

        @pl.when(pair == 0)
        def _():
            pair_in[...] = jnp.zeros_like(pair_in)

        @pl.when(odd == 1)
        def _():
            total_copy(grp).wait_recv()
            both = [join(prior[count, index], total_in[index]) for index in range(per)]

            @pl.when(pair > 0)
            def _():
                pair_copy(1).wait_recv()

            for index in range(per):
                onward[index] = mul(both[index][0], pair_in[index]) + both[index][1]

            @pl.when(pair < last_pair)
            def _():
                pair_copy(2).start()
                pair_copy(1).start()

            for index in range(per):
                entry[index] = apply(total_in[index], pair_in[index])

        @pl.when(odd == 0)
        def _():
            @pl.when(pair > 0)
            def _():
                pair_copy(1).wait_recv()

            entry[...] = pair_in[...]

        def give(step, _):
            shard = lax.rem(me + 1 + step, count)
            for index in range(per):
                starts[shard, index] = apply(prior[shard, index], entry[index])

            @pl.when(shard != me)
            def _():
                down_copy(shard, me).start()

            @pl.when(shard == me)
            def _():
                begin[pl.ds(me * per, per)] = starts[shard]

            return 0

        lax.fori_loop(0, count, give, 0)

    when_owner(compose)
    gate_copy.wait()

    def store(owner):
        span = pl.ds(pl.multiple_of(owner * (per * size), per * size), per * size)
        return pltpu.make_async_copy(o_ref.at[:, span], o_hbm.at[:, span], store_sem.at[owner])

    def finish(step, _):
        owner = lax.rem(me + owners - step, owners) if everyone else step

        @pl.when(owner != me)
        def _():
            down_copy(me, owner).wait_recv()

        for index in range(per):
            head = owner * per + index
            raw = mul(reach[head], begin[head]) + local[head]
            scaled = raw * lax.rsqrt(jnp.mean(raw * raw, axis=-1, keepdims=True) + 1e-05)
            gate = g_ref[:, columns(head)].astype(F32)
            o_ref[:, columns(head)] = (scaled / (1.0 + jnp.exp(-gate))).astype(BF16)
        store(owner).start()
        return 0

    lax.fori_loop(0, owners, finish, 0)

    def drain_up(head, _):
        owner = lax.div(head, per)

        @pl.when(owner != me)
        def _():
            up_copy(head, me, owner).wait_send()

        return 0

    lax.fori_loop(0, heads, drain_up, 0)

    def drain_down():
        @pl.when(odd == 0)
        def _():
            total_copy(grp + 1).wait_send()

        @pl.when(jnp.logical_and(odd == 1, pair < last_pair))
        def _():
            pair_copy(2).wait_send()
            pair_copy(1).wait_send()

        def one(shard, _):
            @pl.when(shard != me)
            def _():
                down_copy(shard, me).wait_send()

            return 0

        lax.fori_loop(0, count, one, 0)

    when_owner(drain_down)

    def drain_store(owner, _):
        store(owner).wait()
        return 0

    lax.fori_loop(0, owners, drain_store, 0)


def shards(groups, count, queries, key_vectors, values, log_decay, write_rate, out_gate):
    seq_count, local_len, features = queries.shape
    heads = write_rate.shape[1]
    size = features // heads
    per = max(heads // count, 1)
    dma = pltpu.SemaphoreType.DMA
    square = (size, size)
    wide = (size, 2 * size)
    call = pl.pallas_call(
        functools.partial(kernel, groups, count, heads),
        out_shape=jax.ShapeDtypeStruct((local_len, features), BF16),
        in_specs=[pl.BlockSpec(memory_space=pltpu.HBM)] * 5
        + [pl.BlockSpec(memory_space=pltpu.VMEM)],
        out_specs=pl.BlockSpec(memory_space=pltpu.HBM),
        scratch_shapes=[pltpu.VMEM((local_len, features), BF16)] * 6
        + [
            pltpu.VMEM((heads, *wide), F32),
            pltpu.VMEM((count, per, *wide), F32),
            pltpu.VMEM((count + 1, per, *wide), F32),
            pltpu.VMEM((per, *wide), F32),
            pltpu.VMEM((per, *square), F32),
            pltpu.VMEM((per, *square), F32),
            pltpu.VMEM((per, *square), F32),
            pltpu.VMEM((count, per, *square), F32),
            pltpu.VMEM((heads, *square), F32),
            pltpu.VMEM((heads, local_len, size), F32),
            pltpu.VMEM((heads, local_len, size), F32),
            dma((4, heads // BATCH)),
            dma,
            dma((heads // per,)),
            dma((heads,)),
            dma((count, per)),
            dma,
            dma,
            dma((2,)),
            dma,
            dma((count,)),
            dma((heads // per,)),
        ],
        compiler_params=pltpu.CompilerParams(
            collective_id=0, has_side_effects=True, vmem_limit_bytes=48 * 1024 * 1024
        ),
        name="delta_attention",
    )
    result = call(
        queries[0], key_vectors[0], values[0], log_decay[0], out_gate[0], write_rate[0]
    )
    return result[None]


def solution(mesh):
    spread = P(None, ("grp", "seq"), None)
    return jax.shard_map(
        functools.partial(shards, mesh.shape["grp"], mesh.shape["seq"]),
        mesh=mesh,
        in_specs=(spread, spread, spread, spread, P(None, None, ("grp", "seq")), spread),
        out_specs=spread,
        check_vma=False,
    )
```

```python
import functools
import jax
import jax.numpy as jnp
from jax import lax
from jax.experimental import pallas as pl
from jax.experimental.pallas import tpu as pltpu
from jax.sharding import PartitionSpec as P

BLOCK = 64
BATCH = 4
MESH = pl.DeviceIdType.MESH
F32 = jnp.float32
BF16 = jnp.bfloat16


def split(value):
    high = value.astype(BF16)
    return high, (value - high.astype(F32)).astype(BF16)


def mul(left, right):
    width = right.shape[1]
    lhs = jnp.concatenate(split(left), axis=1)
    parts = jnp.concatenate(split(right), axis=1)
    out = jnp.dot(lhs, jnp.concatenate([parts, parts], axis=0), preferred_element_type=F32)
    return out[:, :width] + out[:, width:]


def mul_rows(left, right):
    width = right.shape[0]
    lhs = jnp.concatenate(split(left), axis=1)
    parts = jnp.concatenate(split(right), axis=0)
    rhs = jnp.concatenate([parts, parts], axis=1)
    out = lax.dot_general(lhs, rhs, (((1,), (1,)), ((), ())), preferred_element_type=F32)
    return out[:, :width] + out[:, width:]


def mul_wide(left, right):
    high, low = split(left)
    r_high, r_low = split(right)
    lhs = jnp.concatenate([high, low], axis=1)
    rhs = jnp.concatenate([r_high, r_high], axis=0)
    return jnp.dot(lhs, rhs, preferred_element_type=F32) + jnp.dot(
        high, r_low, preferred_element_type=F32
    )


def local_terms(queries, keys, values, decays, rates):
    extent, size = queries[0].shape
    half = extent // 2
    rows = lax.broadcasted_iota(jnp.int32, (extent, extent), 0)
    cols = lax.broadcasted_iota(jnp.int32, (extent, extent), 1)
    same = (rows >= half) == (cols >= half)
    eye = jnp.where(rows == cols, 1.0, 0.0).astype(F32)
    ones = jnp.where(rows >= cols, 1.0, 0.0).astype(BF16)
    cums = [jnp.dot(ones, decay, preferred_element_type=F32) for decay in decays]
    q_f = [query.astype(F32) for query in queries]
    units = []
    for key in keys:
        key_f = key.astype(F32)
        units.append(key_f * lax.rsqrt(jnp.sum(key_f * key_f, axis=-1, keepdims=True) + 1e-06))
    pairs = []
    for query, unit, cum in zip(q_f, units, cums):
        middle = cum[half - 1 : half]
        grow = jnp.exp(cum - middle)
        pairs.append(
            mul_rows(
                jnp.concatenate([unit * grow, query * grow], axis=0), unit * jnp.exp(middle - cum)
            )
        )
    lowers, attends = [], []
    for pair, rate in zip(pairs, rates):
        lowers.append(jnp.where(rows > cols, pair[:extent] * rate, 0.0))
        attends.append(jnp.where(rows >= cols, pair[extent:] * rate, 0.0))
    diag = [jnp.where(same, lower, 0.0) for lower in lowers]
    below = [jnp.where(same, 0.0, lower) for lower in lowers]
    inverse = [eye - part for part in diag]
    power = [mul(part, part) for part in diag]
    for _ in range(half.bit_length() - 3):
        both = [mul(jnp.concatenate([x, p], axis=0), p) for x, p in zip(inverse, power)]
        inverse = [x + b[:extent] for x, b in zip(inverse, both)]
        power = [b[extent:] for b in both]
    inverse = [x + mul(x, p) for x, p in zip(inverse, power)]
    corner = [mul(x[half:], c) for x, c in zip(inverse, below)]
    corner = [mul(c, x) for c, x in zip(corner, inverse)]
    inverse = [
        jnp.concatenate([x[:half], x[half:] - c], axis=0) for x, c in zip(inverse, corner)
    ]
    from_start = [jnp.exp(cum) for cum in cums]
    carry = [
        mul_wide(x, jnp.concatenate([unit * grow, value.astype(F32)], axis=1))
        for x, unit, grow, value in zip(inverse, units, from_start, values)
    ]
    results = []
    for query, unit, cum, grow, attend, rate, carried in zip(
        q_f, units, cums, from_start, attends, rates, carry
    ):
        last = cum[extent - 1 : extent]
        key_end = jnp.transpose(unit * jnp.exp(last - cum)) * rate
        out = mul_wide(jnp.concatenate([attend, key_end], axis=0), carried)
        step_map = jnp.where(rows == cols, jnp.exp(last), 0.0) - out[extent:, :size]
        results.append(
            (
                query * grow - out[:extent, :size],
                out[:extent, size:],
                jnp.concatenate([step_map, out[extent:, size:]], axis=1),
            )
        )
    return results


def kernel(
    groups, count, heads,
    q_hbm, k_hbm, v_hbm, d_hbm, g_hbm, r_ref, o_hbm,
    q_ref, k_ref, v_ref, d_ref, g_ref, o_ref,
    outgo, duo, comp, arrived, prior, total_in, pair_in, entry, onward, starts, slots, begin,
    reach, local,
    load_sem, gate_sem, store_sem, mate_send, mate_recv, up_send, up_recv,
    total_send, total_recv, pair_send, pair_recv, down_send, down_recv, relay_send, relay_recv,
):
    grp, me = lax.axis_index("grp"), lax.axis_index("seq")
    per = max(heads // count, 1)
    owners = heads // per
    size = q_ref.shape[1] // heads
    everyone = owners == count
    places, hosts = count // 2, owners // 2
    place, side = lax.div(me, 2), lax.rem(me, 2)
    mate = me + 1 - 2 * side
    turns = heads // 2 // BATCH
    runs = BATCH // per
    first_turn = lax.div(per * place, BATCH) + 1
    pair, odd = lax.div(grp, 2), lax.rem(grp, 2)
    last_pair = groups // 2 - 1

    def when_owner(body):
        if everyone:
            body()
        else:
            pl.when(me < owners)(body)

    def greet_at(group, seq):
        pl.semaphore_signal(barrier, inc=1, device_id=(group, seq), device_id_type=MESH)

    barrier = pltpu.get_barrier_semaphore()
    greet_at(grp, mate)

    def greet(step, _):
        greet_at(grp, lax.rem(me + 2 * step, count))
        return 0

    lax.fori_loop(1, places, greet, 0)

    @pl.when(odd == 0)
    def _():
        greet_at(grp + 1, me)

    @pl.when(odd == 1)
    def _():
        greet_at(grp - 1, me)

    @pl.when(jnp.logical_and(odd == 0, pair > 0))
    def _():
        greet_at(grp - 1, me)

    @pl.when(jnp.logical_and(odd == 1, pair > 0))
    def _():
        greet_at(grp - 2, me)

    @pl.when(jnp.logical_and(odd == 1, pair < last_pair))
    def _():
        greet_at(grp + 1, me)
        greet_at(grp + 2, me)

    def turn_owners(turn, whose):
        start = lax.rem(turn + first_turn, turns) * runs
        return [2 * (start + run) + whose for run in range(runs)]

    def owner_columns(owner):
        return pl.ds(pl.multiple_of(owner * (per * size), per * size), per * size)

    def load(owner):
        span = owner_columns(owner)
        return [
            pltpu.make_async_copy(far.at[:, span], near.at[:, span], load_sem.at[index, owner])
            for index, (far, near) in enumerate(
                [(d_hbm, d_ref), (k_hbm, k_ref), (q_hbm, q_ref), (v_hbm, v_ref)]
            )
        ]

    for whose in (1 - side, side):
        for turn in range(turns):
            for owner in turn_owners(turn, whose):
                for copy in load(owner):
                    copy.start()
    gate_copy = pltpu.make_async_copy(g_hbm, g_ref, gate_sem)
    gate_copy.start()

    beside = 1 + jnp.minimum(pair, 1) + 2 * odd * jnp.minimum(last_pair - pair, 1)
    pl.semaphore_wait(barrier, places + beside)

    def columns(head):
        return pl.ds(pl.multiple_of(head * size, size), size)

    def join(late, early):
        product = mul_wide(late[:, :size], early)
        return product[:, :size], product[:, size:] + late[:, size:]

    def apply(step, state):
        return mul(step[:, :size], state) + step[:, size:]

    def compute(turn, whose):
        turn_of = turn_owners(turn, whose)
        for owner in turn_of:
            for copy in load(owner):
                copy.wait()
        picked = [owner * per + index for owner in turn_of for index in range(per)]
        places_in = [lax.div(owner, 2) * per + index for owner in turn_of for index in range(per)]
        spans = [columns(head) for head in picked]
        results = local_terms(
            [q_ref[:, span] for span in spans],
            [k_ref[:, span] for span in spans],
            [v_ref[:, span] for span in spans],
            [d_ref[:, span] for span in spans],
            [r_ref[pl.ds(head, 1), :] for head in picked],
        )
        for head, (head_reach, head_local, _step) in zip(picked, results):
            reach[head] = head_reach
            local[head] = head_local
        return places_in, [result[2] for result in results]

    def mate_copy(spot, slot):
        return pltpu.make_async_remote_copy(
            src_ref=outgo.at[spot],
            dst_ref=duo.at[spot, slot],
            send_sem=mate_send.at[spot],
            recv_sem=mate_recv.at[spot],
            device_id=(grp, mate),
            device_id_type=MESH,
        )

    def up_copy(spot, shard, host):
        return pltpu.make_async_remote_copy(
            src_ref=comp.at[spot],
            dst_ref=arrived.at[shard, lax.rem(spot, per)],
            send_sem=up_send.at[spot],
            recv_sem=up_recv.at[shard, lax.rem(spot, per)],
            device_id=(grp, 2 * host + side),
            device_id_type=MESH,
        )

    def for_mate(turn, _):
        spots, steps = compute(turn, 1 - side)
        for spot, step in zip(spots, steps):
            outgo[spot] = step
            mate_copy(spot, side).start()
        return 0

    lax.fori_loop(0, turns, for_mate, 0)

    def for_pair(turn, _):
        spots, steps = compute(turn, side)
        for spot, step in zip(spots, steps):
            duo[spot, side] = step
        for spot in spots:
            mate_copy(spot, 1 - side).wait_recv()
        joined = [join(duo[spot, 1], duo[spot, 0]) for spot in spots]
        for spot, (whole, added) in zip(spots, joined):
            comp[spot, :, :size] = whole
            comp[spot, :, size:] = added
            host = lax.div(spot, per)

            @pl.when(host != place)
            def _():
                up_copy(spot, place, host).start()

            @pl.when(host == place)
            def _():
                arrived[place, lax.rem(spot, per)] = comp[spot]

        return 0

    lax.fori_loop(0, turns, for_pair, 0)

    rows = lax.broadcasted_iota(jnp.int32, (size, 2 * size), 0)
    cols = lax.broadcasted_iota(jnp.int32, (size, 2 * size), 1)

    def total_copy(target):
        return pltpu.make_async_remote_copy(
            src_ref=prior.at[places],
            dst_ref=total_in,
            send_sem=total_send,
            recv_sem=total_recv,
            device_id=(target, me),
            device_id_type=MESH,
        )

    def pair_copy(ahead):
        return pltpu.make_async_remote_copy(
            src_ref=onward,
            dst_ref=pair_in,
            send_sem=pair_send.at[ahead - 1],
            recv_sem=pair_recv,
            device_id=(grp + ahead, me),
            device_id_type=MESH,
        )

    def down_copy(shard, host):
        return pltpu.make_async_remote_copy(
            src_ref=starts.at[shard],
            dst_ref=slots.at[0, pl.ds(host * per, per)],
            send_sem=down_send.at[shard],
            recv_sem=down_recv.at[host],
            device_id=(grp, 2 * shard + side),
            device_id_type=MESH,
        )

    def relay_copy(host):
        return pltpu.make_async_remote_copy(
            src_ref=slots.at[1 - side, pl.ds(host * per, per)],
            dst_ref=begin.at[pl.ds(host * per, per)],
            send_sem=relay_send.at[host],
            recv_sem=relay_recv.at[host],
            device_id=(grp, mate),
            device_id_type=MESH,
        )

    def compose():
        for index in range(per):
            prior[0, index] = jnp.where(rows == cols, 1.0, 0.0).astype(F32)

        def advance(shard, _):
            @pl.when(shard != place)
            def _():
                for index in range(per):
                    up_copy(place * per + index, shard, place).wait_recv()

            for index in range(per):
                whole, added = join(arrived[shard, index], prior[shard, index])
                prior[shard + 1, index, :, :size] = whole
                prior[shard + 1, index, :, size:] = added
            return 0

        lax.fori_loop(0, places, advance, 0)

        @pl.when(odd == 0)
        def _():
            total_copy(grp + 1).start()

        @pl.when(pair == 0)
        def _():
            pair_in[...] = jnp.zeros_like(pair_in)

        @pl.when(odd == 1)
        def _():
            total_copy(grp).wait_recv()
            both = [join(prior[places, index], total_in[index]) for index in range(per)]

            @pl.when(pair > 0)
            def _():
                pair_copy(1).wait_recv()

            for index in range(per):
                onward[index] = mul(both[index][0], pair_in[index]) + both[index][1]

            @pl.when(pair < last_pair)
            def _():
                pair_copy(2).start()
                pair_copy(1).start()

            for index in range(per):
                entry[index] = apply(total_in[index], pair_in[index])

        @pl.when(odd == 0)
        def _():
            @pl.when(pair > 0)
            def _():
                pair_copy(1).wait_recv()

            entry[...] = pair_in[...]

        def give(step, _):
            shard = lax.rem(place + 1 + step, places)
            for index in range(per):
                starts[shard, index] = apply(prior[shard, index], entry[index])

            @pl.when(shard != place)
            def _():
                down_copy(shard, place).start()

            @pl.when(shard == place)
            def _():
                slots[0, pl.ds(place * per, per)] = starts[shard]

            return 0

        lax.fori_loop(0, places, give, 0)

    when_owner(compose)
    gate_copy.wait()

    def store(owner):
        span = owner_columns(owner)
        return pltpu.make_async_copy(o_ref.at[:, span], o_hbm.at[:, span], store_sem.at[owner])

    def finish(owner, states):
        for index in range(per):
            head = owner * per + index
            raw = mul(reach[head], states[index]) + local[head]
            scaled = raw * lax.rsqrt(jnp.mean(raw * raw, axis=-1, keepdims=True) + 1e-05)
            gate = g_ref[:, columns(head)].astype(F32)
            o_ref[:, columns(head)] = (scaled / (1.0 + jnp.exp(-gate))).astype(BF16)
        store(owner).start()

    def nearest(step):
        return lax.rem(place + hosts - step, hosts) if everyone else step

    def relay(step, _):
        host = nearest(step)

        @pl.when(host != place)
        def _():
            down_copy(place, host).wait_recv()

        for index in range(per):
            spot = host * per + index
            slots[1, spot] = apply(duo[spot, 0], slots[0, spot])
        relay_copy(host).start()
        finish(2 * host + side, [slots[side, host * per + index] for index in range(per)])
        return 0

    lax.fori_loop(0, hosts, relay, 0)

    def last(step, _):
        host = nearest(step)
        relay_copy(host).wait_recv()
        finish(2 * host + 1 - side, [begin[host * per + index] for index in range(per)])
        return 0

    lax.fori_loop(0, hosts, last, 0)

    def drain(spot, _):
        mate_copy(spot, side).wait_send()
        host = lax.div(spot, per)

        @pl.when(host != place)
        def _():
            up_copy(spot, place, host).wait_send()

        return 0

    lax.fori_loop(0, heads // 2, drain, 0)

    def drain_down():
        @pl.when(odd == 0)
        def _():
            total_copy(grp + 1).wait_send()

        @pl.when(jnp.logical_and(odd == 1, pair < last_pair))
        def _():
            pair_copy(2).wait_send()
            pair_copy(1).wait_send()

        def one(shard, _):
            @pl.when(shard != place)
            def _():
                down_copy(shard, place).wait_send()

            return 0

        lax.fori_loop(0, places, one, 0)

    when_owner(drain_down)

    def drain_relay(host, _):
        relay_copy(host).wait_send()
        return 0

    lax.fori_loop(0, hosts, drain_relay, 0)

    def drain_store(owner, _):
        store(owner).wait()
        return 0

    lax.fori_loop(0, owners, drain_store, 0)


def shards(groups, count, queries, key_vectors, values, log_decay, write_rate, out_gate):
    seq_count, local_len, features = queries.shape
    heads = write_rate.shape[1]
    size = features // heads
    per = max(heads // count, 1)
    owners = heads // per
    half, places, hosts = heads // 2, count // 2, owners // 2
    dma = pltpu.SemaphoreType.DMA
    square = (size, size)
    wide = (size, 2 * size)
    call = pl.pallas_call(
        functools.partial(kernel, groups, count, heads),
        out_shape=jax.ShapeDtypeStruct((local_len, features), BF16),
        in_specs=[pl.BlockSpec(memory_space=pltpu.HBM)] * 5
        + [pl.BlockSpec(memory_space=pltpu.VMEM)],
        out_specs=pl.BlockSpec(memory_space=pltpu.HBM),
        scratch_shapes=[pltpu.VMEM((local_len, features), BF16)] * 6
        + [
            pltpu.VMEM((half, *wide), F32),
            pltpu.VMEM((half, 2, *wide), F32),
            pltpu.VMEM((half, *wide), F32),
            pltpu.VMEM((places, per, *wide), F32),
            pltpu.VMEM((places + 1, per, *wide), F32),
            pltpu.VMEM((per, *wide), F32),
            pltpu.VMEM((per, *square), F32),
            pltpu.VMEM((per, *square), F32),
            pltpu.VMEM((per, *square), F32),
            pltpu.VMEM((places, per, *square), F32),
            pltpu.VMEM((2, half, *square), F32),
            pltpu.VMEM((half, *square), F32),
            pltpu.VMEM((heads, local_len, size), F32),
            pltpu.VMEM((heads, local_len, size), F32),
            dma((4, owners)),
            dma,
            dma((owners,)),
            dma((half,)),
            dma((half,)),
            dma((half,)),
            dma((places, per)),
            dma,
            dma,
            dma((2,)),
            dma,
            dma((places,)),
            dma((hosts,)),
            dma((hosts,)),
            dma((hosts,)),
        ],
        compiler_params=pltpu.CompilerParams(
            collective_id=0, has_side_effects=True, vmem_limit_bytes=63 * 1024 * 1024
        ),
        name="delta_attention",
    )
    result = call(
        queries[0], key_vectors[0], values[0], log_decay[0], out_gate[0], write_rate[0]
    )
    return result[None]


def solution(mesh):
    spread = P(None, ("grp", "seq"), None)
    return jax.shard_map(
        functools.partial(shards, mesh.shape["grp"], mesh.shape["seq"]),
        mesh=mesh,
        in_specs=(spread, spread, spread, spread, P(None, None, ("grp", "seq")), spread),
        out_specs=spread,
        check_vma=False,
    )
```

```python
import functools
import jax
import jax.numpy as jnp
from jax import lax
from jax.experimental import pallas as pl
from jax.experimental.pallas import tpu as pltpu
from jax.sharding import PartitionSpec as P

BLOCK = 64
BATCH = 4
MESH = pl.DeviceIdType.MESH
F32 = jnp.float32
BF16 = jnp.bfloat16


def split(value):
    high = value.astype(BF16)
    return high, (value - high.astype(F32)).astype(BF16)


def mul(left, right):
    width = right.shape[1]
    lhs = jnp.concatenate(split(left), axis=1)
    parts = jnp.concatenate(split(right), axis=1)
    out = jnp.dot(lhs, jnp.concatenate([parts, parts], axis=0), preferred_element_type=F32)
    return out[:, :width] + out[:, width:]


def mul_split(left, right):
    width = right[0].shape[1]
    parts = jnp.concatenate(right, axis=1)
    out = jnp.dot(
        jnp.concatenate(left, axis=1),
        jnp.concatenate([parts, parts], axis=0),
        preferred_element_type=F32,
    )
    return out[:, :width] + out[:, width:]


def mul_rows(left, right):
    width = right.shape[0]
    lhs = jnp.concatenate(split(left), axis=1)
    parts = jnp.concatenate(split(right), axis=0)
    rhs = jnp.concatenate([parts, parts], axis=1)
    out = lax.dot_general(lhs, rhs, (((1,), (1,)), ((), ())), preferred_element_type=F32)
    return out[:, :width] + out[:, width:]


def mul_wide(left, right):
    high, low = split(left)
    r_high, r_low = split(right)
    lhs = jnp.concatenate([high, low], axis=1)
    rhs = jnp.concatenate([r_high, r_high], axis=0)
    return jnp.dot(lhs, rhs, preferred_element_type=F32) + jnp.dot(
        high, r_low, preferred_element_type=F32
    )


def mul_both(upper, lower, right):
    width = right[0].shape[1]
    lhs = jnp.concatenate(
        [jnp.concatenate([up, low], axis=0) for up, low in zip(upper, lower)], axis=1
    )
    parts = jnp.concatenate(right, axis=1)
    out = jnp.dot(lhs, jnp.concatenate([parts, parts], axis=0), preferred_element_type=F32)
    return out[:, :width] + out[:, width:]


def state_terms(keys, values, decays, rates):
    extent, size = keys[0].shape
    half = extent // 2
    rows = lax.broadcasted_iota(jnp.int32, (extent, extent), 0)
    cols = lax.broadcasted_iota(jnp.int32, (extent, extent), 1)
    same = (rows >= half) == (cols >= half)
    eye = jnp.where(rows == cols, 1.0, 0.0).astype(F32)
    ones = jnp.where(rows >= cols, 1.0, 0.0).astype(BF16)
    cums = [jnp.dot(ones, decay, preferred_element_type=F32) for decay in decays]
    units = []
    for key in keys:
        key_f = key.astype(F32)
        units.append(key_f * lax.rsqrt(jnp.sum(key_f * key_f, axis=-1, keepdims=True) + 1e-06))
    shrunk = [unit * jnp.exp(cum[half - 1 : half] - cum) for unit, cum in zip(units, cums)]
    pairs = [
        mul_rows(unit * jnp.exp(cum - cum[half - 1 : half]), shrink)
        for unit, cum, shrink in zip(units, cums, shrunk)
    ]
    lowers = [jnp.where(rows > cols, product * rate, 0.0) for product, rate in zip(pairs, rates)]
    diag = [jnp.where(same, lower, 0.0) for lower in lowers]
    below = [jnp.where(same, 0.0, lower) for lower in lowers]
    inverse = [eye - part for part in diag]
    power = [split(mul(part, part)) for part in diag]
    for _ in range(half.bit_length() - 3):
        both = [mul_both(split(x), p, p) for x, p in zip(inverse, power)]
        inverse = [x + b[:extent] for x, b in zip(inverse, both)]
        power = [split(b[extent:]) for b in both]
    inverse = [x + mul_split(split(x), p) for x, p in zip(inverse, power)]
    corner = [mul(x[half:], c) for x, c in zip(inverse, below)]
    corner = [mul(c, x) for c, x in zip(corner, inverse)]
    inverse = [
        jnp.concatenate([x[:half], x[half:] - c], axis=0) for x, c in zip(inverse, corner)
    ]
    carry = [
        mul_wide(x, jnp.concatenate([unit * jnp.exp(cum), value.astype(F32)], axis=1))
        for x, unit, cum, value in zip(inverse, units, cums, values)
    ]
    steps = []
    for unit, cum, rate, carried in zip(units, cums, rates, carry):
        last = cum[extent - 1 : extent]
        key_end = jnp.transpose(unit * jnp.exp(last - cum)) * rate
        out = mul_wide(key_end, carried)
        step_map = jnp.where(rows == cols, jnp.exp(last), 0.0) - out[:, :size]
        steps.append(jnp.concatenate([step_map, out[:, size:]], axis=1))
    return cums, shrunk, carry, steps


def output_terms(queries, cums, shrunk, carry, rates):
    extent, size = queries[0].shape
    half = extent // 2
    rows = lax.broadcasted_iota(jnp.int32, (extent, extent), 0)
    cols = lax.broadcasted_iota(jnp.int32, (extent, extent), 1)
    q_f = [query.astype(F32) for query in queries]
    pairs = [
        mul_rows(query * jnp.exp(cum - cum[half - 1 : half]), shrink)
        for query, cum, shrink in zip(q_f, cums, shrunk)
    ]
    attends = [jnp.where(rows >= cols, product * rate, 0.0) for product, rate in zip(pairs, rates)]
    outs = [mul_wide(attend, carried) for attend, carried in zip(attends, carry)]
    return [
        (query * jnp.exp(cum) - out[:, :size], out[:, size:])
        for query, cum, out in zip(q_f, cums, outs)
    ]


def kernel(
    groups, count, heads,
    q_hbm, k_hbm, v_hbm, d_hbm, g_hbm, r_ref, o_ref,
    q_ref, k_ref, v_ref, d_ref, g_ref,
    outgo, duo, comp, arrived, prior, total_in, pair_in, entry, onward, starts, slots, begin,
    reach, local, kept_cum, kept_key, kept_carry,
    load_sem, query_sem, gate_sem, mate_send, mate_recv, up_send, up_recv,
    total_send, total_recv, pair_send, pair_recv, down_send, down_recv, relay_send, relay_recv,
):
    grp, me = lax.axis_index("grp"), lax.axis_index("seq")
    per = max(heads // count, 1)
    owners = heads // per
    size = q_ref.shape[1] // heads
    everyone = owners == count
    places, hosts = count // 2, owners // 2
    place, side = lax.div(me, 2), lax.rem(me, 2)
    mate = me + 1 - 2 * side
    turns = heads // 2 // BATCH
    runs = BATCH // per
    first_turn = lax.div(per * place, BATCH) + 1
    pair, odd = lax.div(grp, 2), lax.rem(grp, 2)
    last_pair = groups // 2 - 1

    def when_owner(body):
        if everyone:
            body()
        else:
            pl.when(me < owners)(body)

    def greet_at(group, seq):
        pl.semaphore_signal(barrier, inc=1, device_id=(group, seq), device_id_type=MESH)

    barrier = pltpu.get_barrier_semaphore()
    greet_at(grp, mate)

    def greet(step, _):
        greet_at(grp, lax.rem(me + 2 * step, count))
        return 0

    lax.fori_loop(1, places, greet, 0)

    @pl.when(odd == 0)
    def _():
        greet_at(grp + 1, me)

    @pl.when(odd == 1)
    def _():
        greet_at(grp - 1, me)

    @pl.when(jnp.logical_and(odd == 0, pair > 0))
    def _():
        greet_at(grp - 1, me)

    @pl.when(jnp.logical_and(odd == 1, pair > 0))
    def _():
        greet_at(grp - 2, me)

    @pl.when(jnp.logical_and(odd == 1, pair < last_pair))
    def _():
        greet_at(grp + 1, me)
        greet_at(grp + 2, me)

    def turn_owners(turn, whose):
        start = lax.rem(turn + first_turn, turns) * runs
        return [2 * (start + run) + whose for run in range(runs)]

    def owner_columns(owner):
        return pl.ds(pl.multiple_of(owner * (per * size), per * size), per * size)

    def load(owner):
        span = owner_columns(owner)
        return [
            pltpu.make_async_copy(far.at[:, span], near.at[:, span], load_sem.at[index, owner])
            for index, (far, near) in enumerate(
                [(d_hbm, d_ref), (k_hbm, k_ref), (v_hbm, v_ref)]
            )
        ]

    for whose in (1 - side, side):
        for turn in range(turns):
            for owner in turn_owners(turn, whose):
                for copy in load(owner):
                    copy.start()
    query_copy = pltpu.make_async_copy(q_hbm, q_ref, query_sem)
    query_copy.start()
    gate_copy = pltpu.make_async_copy(g_hbm, g_ref, gate_sem)
    gate_copy.start()

    beside = 1 + jnp.minimum(pair, 1) + 2 * odd * jnp.minimum(last_pair - pair, 1)
    pl.semaphore_wait(barrier, places + beside)

    def columns(head):
        return pl.ds(pl.multiple_of(head * size, size), size)

    def join(late, early):
        product = mul_wide(late[:, :size], early)
        return product[:, :size], product[:, size:] + late[:, size:]

    def apply(step, state):
        return mul(step[:, :size], state) + step[:, size:]

    def compute(turn, whose):
        turn_of = turn_owners(turn, whose)
        for owner in turn_of:
            for copy in load(owner):
                copy.wait()
        picked = [owner * per + index for owner in turn_of for index in range(per)]
        places_in = [lax.div(owner, 2) * per + index for owner in turn_of for index in range(per)]
        spans = [columns(head) for head in picked]
        cums, shrunk, carry, steps = state_terms(
            [k_ref[:, span] for span in spans],
            [v_ref[:, span] for span in spans],
            [d_ref[:, span] for span in spans],
            [r_ref[pl.ds(head, 1), :] for head in picked],
        )
        for head, cum, shrink, carried in zip(picked, cums, shrunk, carry):
            kept_cum[head] = cum
            kept_key[head] = shrink
            kept_carry[head] = carried
        return places_in, steps

    def outputs(batch, _):
        picked = [batch * BATCH + index for index in range(BATCH)]
        results = output_terms(
            [q_ref[:, columns(head)] for head in picked],
            [kept_cum[head] for head in picked],
            [kept_key[head] for head in picked],
            [kept_carry[head] for head in picked],
            [r_ref[pl.ds(head, 1), :] for head in picked],
        )
        for head, (head_reach, head_local) in zip(picked, results):
            reach[head] = head_reach
            local[head] = head_local
        return 0

    def mate_copy(spot, slot):
        return pltpu.make_async_remote_copy(
            src_ref=outgo.at[spot],
            dst_ref=duo.at[spot, slot],
            send_sem=mate_send.at[spot],
            recv_sem=mate_recv.at[spot],
            device_id=(grp, mate),
            device_id_type=MESH,
        )

    def up_copy(spot, shard, host):
        return pltpu.make_async_remote_copy(
            src_ref=comp.at[spot],
            dst_ref=arrived.at[shard, lax.rem(spot, per)],
            send_sem=up_send.at[spot],
            recv_sem=up_recv.at[shard, lax.rem(spot, per)],
            device_id=(grp, 2 * host + side),
            device_id_type=MESH,
        )

    def for_mate(turn, _):
        spots, steps = compute(turn, 1 - side)
        for spot, step in zip(spots, steps):
            outgo[spot] = step
            mate_copy(spot, side).start()
        return 0

    lax.fori_loop(0, turns, for_mate, 0)

    def for_pair(turn, _):
        spots, steps = compute(turn, side)
        for spot, step in zip(spots, steps):
            duo[spot, side] = step
        for spot in spots:
            mate_copy(spot, 1 - side).wait_recv()
        joined = [join(duo[spot, 1], duo[spot, 0]) for spot in spots]
        for spot, (whole, added) in zip(spots, joined):
            comp[spot, :, :size] = whole
            comp[spot, :, size:] = added
            host = lax.div(spot, per)

            @pl.when(host != place)
            def _():
                up_copy(spot, place, host).start()

            @pl.when(host == place)
            def _():
                arrived[place, lax.rem(spot, per)] = comp[spot]

        return 0

    lax.fori_loop(0, turns, for_pair, 0)

    rows = lax.broadcasted_iota(jnp.int32, (size, 2 * size), 0)
    cols = lax.broadcasted_iota(jnp.int32, (size, 2 * size), 1)

    def total_copy(target):
        return pltpu.make_async_remote_copy(
            src_ref=prior.at[places],
            dst_ref=total_in,
            send_sem=total_send,
            recv_sem=total_recv,
            device_id=(target, me),
            device_id_type=MESH,
        )

    def pair_copy(ahead):
        return pltpu.make_async_remote_copy(
            src_ref=onward,
            dst_ref=pair_in,
            send_sem=pair_send.at[ahead - 1],
            recv_sem=pair_recv,
            device_id=(grp + ahead, me),
            device_id_type=MESH,
        )

    def down_copy(shard, host):
        return pltpu.make_async_remote_copy(
            src_ref=starts.at[shard],
            dst_ref=slots.at[0, pl.ds(host * per, per)],
            send_sem=down_send.at[shard],
            recv_sem=down_recv.at[host],
            device_id=(grp, 2 * shard + side),
            device_id_type=MESH,
        )

    def relay_copy(host):
        return pltpu.make_async_remote_copy(
            src_ref=slots.at[1 - side, pl.ds(host * per, per)],
            dst_ref=begin.at[pl.ds(host * per, per)],
            send_sem=relay_send.at[host],
            recv_sem=relay_recv.at[host],
            device_id=(grp, mate),
            device_id_type=MESH,
        )

    def compose():
        for index in range(per):
            prior[0, index] = jnp.where(rows == cols, 1.0, 0.0).astype(F32)

        def advance(shard, _):
            @pl.when(shard != place)
            def _():
                for index in range(per):
                    up_copy(place * per + index, shard, place).wait_recv()

            for index in range(per):
                whole, added = join(arrived[shard, index], prior[shard, index])
                prior[shard + 1, index, :, :size] = whole
                prior[shard + 1, index, :, size:] = added
            return 0

        lax.fori_loop(0, places, advance, 0)

        @pl.when(odd == 0)
        def _():
            total_copy(grp + 1).start()

        @pl.when(pair == 0)
        def _():
            pair_in[...] = jnp.zeros_like(pair_in)

        @pl.when(odd == 1)
        def _():
            total_copy(grp).wait_recv()
            both = [join(prior[places, index], total_in[index]) for index in range(per)]

            @pl.when(pair > 0)
            def _():
                pair_copy(1).wait_recv()

            for index in range(per):
                onward[index] = mul(both[index][0], pair_in[index]) + both[index][1]

            @pl.when(pair < last_pair)
            def _():
                pair_copy(2).start()
                pair_copy(1).start()

            for index in range(per):
                entry[index] = apply(total_in[index], pair_in[index])

        @pl.when(odd == 0)
        def _():
            @pl.when(pair > 0)
            def _():
                pair_copy(1).wait_recv()

            entry[...] = pair_in[...]

        def give(step, _):
            shard = lax.rem(place + 1 + step, places)
            for index in range(per):
                starts[shard, index] = apply(prior[shard, index], entry[index])

            @pl.when(shard != place)
            def _():
                down_copy(shard, place).start()

            @pl.when(shard == place)
            def _():
                slots[0, pl.ds(place * per, per)] = starts[shard]

            return 0

        lax.fori_loop(0, places, give, 0)

    batches = heads // BATCH
    query_copy.wait()
    lax.fori_loop(0, batches // 2, outputs, 0)
    when_owner(compose)
    lax.fori_loop(batches // 2, batches, outputs, 0)
    gate_copy.wait()

    def finish(owner, states):
        for index in range(per):
            head = owner * per + index
            raw = mul(reach[head], states[index]) + local[head]
            scaled = raw * lax.rsqrt(jnp.mean(raw * raw, axis=-1, keepdims=True) + 1e-05)
            gate = g_ref[:, columns(head)].astype(F32)
            o_ref[:, columns(head)] = (scaled / (1.0 + jnp.exp(-gate))).astype(BF16)

    def nearest(step):
        return lax.rem(place + hosts - step, hosts) if everyone else step

    def relay(step, _):
        host = nearest(step)

        @pl.when(host != place)
        def _():
            down_copy(place, host).wait_recv()

        for index in range(per):
            spot = host * per + index
            slots[1, spot] = apply(duo[spot, 0], slots[0, spot])
        relay_copy(host).start()
        finish(2 * host + side, [slots[side, host * per + index] for index in range(per)])
        return 0

    lax.fori_loop(0, hosts, relay, 0)

    def last(step, _):
        host = nearest(step)
        relay_copy(host).wait_recv()
        finish(2 * host + 1 - side, [begin[host * per + index] for index in range(per)])
        return 0

    lax.fori_loop(0, hosts, last, 0)

    def drain(spot, _):
        mate_copy(spot, side).wait_send()
        host = lax.div(spot, per)

        @pl.when(host != place)
        def _():
            up_copy(spot, place, host).wait_send()

        return 0

    lax.fori_loop(0, heads // 2, drain, 0)

    def drain_down():
        @pl.when(odd == 0)
        def _():
            total_copy(grp + 1).wait_send()

        @pl.when(jnp.logical_and(odd == 1, pair < last_pair))
        def _():
            pair_copy(2).wait_send()
            pair_copy(1).wait_send()

        def one(shard, _):
            @pl.when(shard != place)
            def _():
                down_copy(shard, place).wait_send()

            return 0

        lax.fori_loop(0, places, one, 0)

    when_owner(drain_down)

    def drain_relay(host, _):
        relay_copy(host).wait_send()
        return 0

    lax.fori_loop(0, hosts, drain_relay, 0)


def shards(groups, count, queries, key_vectors, values, log_decay, write_rate, out_gate):
    seq_count, local_len, features = queries.shape
    heads = write_rate.shape[1]
    size = features // heads
    per = max(heads // count, 1)
    owners = heads // per
    half, places, hosts = heads // 2, count // 2, owners // 2
    dma = pltpu.SemaphoreType.DMA
    square = (size, size)
    wide = (size, 2 * size)
    call = pl.pallas_call(
        functools.partial(kernel, groups, count, heads),
        out_shape=jax.ShapeDtypeStruct((local_len, features), BF16),
        in_specs=[pl.BlockSpec(memory_space=pltpu.HBM)] * 5
        + [pl.BlockSpec(memory_space=pltpu.VMEM)],
        out_specs=pl.BlockSpec(memory_space=pltpu.VMEM),
        scratch_shapes=[pltpu.VMEM((local_len, features), BF16)] * 5
        + [
            pltpu.VMEM((half, *wide), F32),
            pltpu.VMEM((half, 2, *wide), F32),
            pltpu.VMEM((half, *wide), F32),
            pltpu.VMEM((places, per, *wide), F32),
            pltpu.VMEM((places + 1, per, *wide), F32),
            pltpu.VMEM((per, *wide), F32),
            pltpu.VMEM((per, *square), F32),
            pltpu.VMEM((per, *square), F32),
            pltpu.VMEM((per, *square), F32),
            pltpu.VMEM((places, per, *square), F32),
            pltpu.VMEM((2, half, *square), F32),
            pltpu.VMEM((half, *square), F32),
            pltpu.VMEM((heads, local_len, size), F32),
            pltpu.VMEM((heads, local_len, size), F32),
            pltpu.VMEM((heads, local_len, size), F32),
            pltpu.VMEM((heads, local_len, size), F32),
            pltpu.VMEM((heads, local_len, 2 * size), F32),
            dma((3, owners)),
            dma,
            dma,
            dma((half,)),
            dma((half,)),
            dma((half,)),
            dma((places, per)),
            dma,
            dma,
            dma((2,)),
            dma,
            dma((places,)),
            dma((hosts,)),
            dma((hosts,)),
            dma((hosts,)),
        ],
        compiler_params=pltpu.CompilerParams(
            collective_id=0, has_side_effects=True, vmem_limit_bytes=63 * 1024 * 1024
        ),
        name="delta_attention",
    )
    result = call(
        queries[0], key_vectors[0], values[0], log_decay[0], out_gate[0], write_rate[0]
    )
    return result[None]


def solution(mesh):
    spread = P(None, ("grp", "seq"), None)
    return jax.shard_map(
        functools.partial(shards, mesh.shape["grp"], mesh.shape["seq"]),
        mesh=mesh,
        in_specs=(spread, spread, spread, spread, P(None, None, ("grp", "seq")), spread),
        out_specs=spread,
        check_vma=False,
    )
```

```python
import functools
import jax
import jax.numpy as jnp
from jax import lax
from jax.experimental import pallas as pl
from jax.experimental.pallas import tpu as pltpu
from jax.sharding import PartitionSpec as P

BLOCK = 64
BATCH = 2
MESH = pl.DeviceIdType.MESH
F32 = jnp.float32
BF16 = jnp.bfloat16


def split(value):
    high = value.astype(BF16)
    return high, (value - high.astype(F32)).astype(BF16)


def mul(left, right):
    width = right.shape[1]
    lhs = jnp.concatenate(split(left), axis=1)
    parts = jnp.concatenate(split(right), axis=1)
    out = jnp.dot(lhs, jnp.concatenate([parts, parts], axis=0), preferred_element_type=F32)
    return out[:, :width] + out[:, width:]


def mul_split(left, right):
    width = right[0].shape[1]
    parts = jnp.concatenate(right, axis=1)
    out = jnp.dot(
        jnp.concatenate(left, axis=1),
        jnp.concatenate([parts, parts], axis=0),
        preferred_element_type=F32,
    )
    return out[:, :width] + out[:, width:]


def mul_rows(left, right):
    width = right.shape[0]
    lhs = jnp.concatenate(split(left), axis=1)
    parts = jnp.concatenate(split(right), axis=0)
    rhs = jnp.concatenate([parts, parts], axis=1)
    out = lax.dot_general(lhs, rhs, (((1,), (1,)), ((), ())), preferred_element_type=F32)
    return out[:, :width] + out[:, width:]


def mul_wide(left, right):
    high, low = split(left)
    r_high, r_low = split(right)
    lhs = jnp.concatenate([high, low], axis=1)
    rhs = jnp.concatenate([r_high, r_high], axis=0)
    return jnp.dot(lhs, rhs, preferred_element_type=F32) + jnp.dot(
        high, r_low, preferred_element_type=F32
    )


def mul_both(upper, lower, right):
    width = right[0].shape[1]
    lhs = jnp.concatenate(
        [jnp.concatenate([up, low], axis=0) for up, low in zip(upper, lower)], axis=1
    )
    parts = jnp.concatenate(right, axis=1)
    out = jnp.dot(lhs, jnp.concatenate([parts, parts], axis=0), preferred_element_type=F32)
    return out[:, :width] + out[:, width:]


def state_terms(keys, values, decays, rates):
    extent, size = keys[0].shape
    half = extent // 2
    rows = lax.broadcasted_iota(jnp.int32, (extent, extent), 0)
    cols = lax.broadcasted_iota(jnp.int32, (extent, extent), 1)
    same = (rows >= half) == (cols >= half)
    eye = jnp.where(rows == cols, 1.0, 0.0).astype(F32)
    ones = jnp.where(rows >= cols, 1.0, 0.0).astype(BF16)
    cums = [jnp.dot(ones, decay, preferred_element_type=F32) for decay in decays]
    units = []
    for key in keys:
        key_f = key.astype(F32)
        units.append(key_f * lax.rsqrt(jnp.sum(key_f * key_f, axis=-1, keepdims=True) + 1e-06))
    shrunk = [unit * jnp.exp(cum[half - 1 : half] - cum) for unit, cum in zip(units, cums)]
    pairs = [
        mul_rows(unit * jnp.exp(cum - cum[half - 1 : half]), shrink)
        for unit, cum, shrink in zip(units, cums, shrunk)
    ]
    lowers = [jnp.where(rows > cols, product * rate, 0.0) for product, rate in zip(pairs, rates)]
    diag = [jnp.where(same, lower, 0.0) for lower in lowers]
    below = [jnp.where(same, 0.0, lower) for lower in lowers]
    inverse = [eye - part for part in diag]
    power = [split(mul(part, part)) for part in diag]
    for _ in range(half.bit_length() - 3):
        both = [mul_both(split(x), p, p) for x, p in zip(inverse, power)]
        inverse = [x + b[:extent] for x, b in zip(inverse, both)]
        power = [split(b[extent:]) for b in both]
    inverse = [x + mul_split(split(x), p) for x, p in zip(inverse, power)]
    corner = [mul(x[half:], c) for x, c in zip(inverse, below)]
    corner = [mul(c, x) for c, x in zip(corner, inverse)]
    inverse = [
        jnp.concatenate([x[:half], x[half:] - c], axis=0) for x, c in zip(inverse, corner)
    ]
    carry = [
        mul_wide(x, jnp.concatenate([unit * jnp.exp(cum), value.astype(F32)], axis=1))
        for x, unit, cum, value in zip(inverse, units, cums, values)
    ]
    steps = []
    for unit, cum, rate, carried in zip(units, cums, rates, carry):
        last = cum[extent - 1 : extent]
        key_end = jnp.transpose(unit * jnp.exp(last - cum)) * rate
        out = mul_wide(key_end, carried)
        step_map = jnp.where(rows == cols, jnp.exp(last), 0.0) - out[:, :size]
        steps.append(jnp.concatenate([step_map, out[:, size:]], axis=1))
    return cums, shrunk, carry, steps


def output_terms(queries, cums, shrunk, carry, rates):
    extent, size = queries[0].shape
    half = extent // 2
    rows = lax.broadcasted_iota(jnp.int32, (extent, extent), 0)
    cols = lax.broadcasted_iota(jnp.int32, (extent, extent), 1)
    q_f = [query.astype(F32) for query in queries]
    pairs = [
        mul_rows(query * jnp.exp(cum - cum[half - 1 : half]), shrink)
        for query, cum, shrink in zip(q_f, cums, shrunk)
    ]
    attends = [jnp.where(rows >= cols, product * rate, 0.0) for product, rate in zip(pairs, rates)]
    outs = [mul_wide(attend, carried) for attend, carried in zip(attends, carry)]
    return [
        (query * jnp.exp(cum) - out[:, :size], out[:, size:])
        for query, cum, out in zip(q_f, cums, outs)
    ]


def flip(own, high, low):
    return 2 * lax.rem(lax.div(own, 2) + high, 2) + lax.rem(lax.rem(own, 2) + low, 2)


def far_first(step, own, extent):
    if extent != 4:
        return lax.rem(own + 1 + step, extent)
    late = lax.div(step, 2)
    return flip(own, 1 - late, lax.rem(step + late, 2))


def near_first(step, own, extent):
    if extent != 4:
        return lax.rem(own + extent - step, extent)
    return flip(own, lax.div(step, 2), lax.rem(step, 2))


def kernel(
    groups, count, heads,
    q_hbm, k_hbm, v_hbm, d_hbm, g_hbm, r_ref, o_ref,
    q_ref, k_ref, v_ref, d_ref, g_ref,
    outgo, duo, comp, arrived, prior, total_in, pair_in, entry, onward, starts, slots, begin,
    reach, local, kept_cum, kept_key, kept_carry,
    load_sem, query_sem, gate_sem, mate_send, mate_recv, up_send, up_recv,
    total_send, total_recv, pair_send, pair_recv, down_send, down_recv, relay_send, relay_recv,
):
    grp, me = lax.axis_index("grp"), lax.axis_index("seq")
    per = max(heads // count, 1)
    owners = heads // per
    size = q_ref.shape[1] // heads
    everyone = owners == count
    places, hosts = count // 2, owners // 2
    place, side = lax.div(me, 2), lax.rem(me, 2)
    mate = me + 1 - 2 * side
    turns = heads // 2 // BATCH
    runs = BATCH // per
    own_turn = lax.rem(lax.div(per * place, BATCH), turns)
    pair, odd = lax.div(grp, 2), lax.rem(grp, 2)
    last_pair = groups // 2 - 1

    def when_owner(body):
        if everyone:
            body()
        else:
            pl.when(me < owners)(body)

    def greet_at(group, seq):
        pl.semaphore_signal(barrier, inc=1, device_id=(group, seq), device_id_type=MESH)

    barrier = pltpu.get_barrier_semaphore()
    greet_at(grp, mate)

    def greet(step, _):
        greet_at(grp, lax.rem(me + 2 * step, count))
        return 0

    lax.fori_loop(1, places, greet, 0)

    @pl.when(odd == 0)
    def _():
        greet_at(grp + 1, me)

    @pl.when(odd == 1)
    def _():
        greet_at(grp - 1, me)

    @pl.when(jnp.logical_and(odd == 0, pair > 0))
    def _():
        greet_at(grp - 1, me)

    @pl.when(jnp.logical_and(odd == 1, pair > 0))
    def _():
        greet_at(grp - 2, me)

    @pl.when(jnp.logical_and(odd == 1, pair < last_pair))
    def _():
        greet_at(grp + 1, me)
        greet_at(grp + 2, me)

    def turn_owners(turn, whose):
        start = far_first(jnp.int32(turn), own_turn, turns) * runs
        return [2 * (start + run) + whose for run in range(runs)]

    def owner_columns(owner):
        return pl.ds(pl.multiple_of(owner * (per * size), per * size), per * size)

    def load(owner):
        span = owner_columns(owner)
        return [
            pltpu.make_async_copy(far.at[:, span], near.at[:, span], load_sem.at[index, owner])
            for index, (far, near) in enumerate(
                [(d_hbm, d_ref), (k_hbm, k_ref), (v_hbm, v_ref)]
            )
        ]

    for whose in (1 - side, side):
        for turn in range(turns):
            for owner in turn_owners(turn, whose):
                for copy in load(owner):
                    copy.start()
    query_copy = pltpu.make_async_copy(q_hbm, q_ref, query_sem)
    query_copy.start()
    gate_copy = pltpu.make_async_copy(g_hbm, g_ref, gate_sem)
    gate_copy.start()

    beside = 1 + jnp.minimum(pair, 1) + 2 * odd * jnp.minimum(last_pair - pair, 1)
    pl.semaphore_wait(barrier, places + beside)

    def columns(head):
        return pl.ds(pl.multiple_of(head * size, size), size)

    def join(late, early):
        product = mul_wide(late[:, :size], early)
        return product[:, :size], product[:, size:] + late[:, size:]

    def apply(step, state):
        return mul(step[:, :size], state) + step[:, size:]

    def compute(turn, whose):
        turn_of = turn_owners(turn, whose)
        for owner in turn_of:
            for copy in load(owner):
                copy.wait()
        picked = [owner * per + index for owner in turn_of for index in range(per)]
        places_in = [lax.div(owner, 2) * per + index for owner in turn_of for index in range(per)]
        spans = [columns(head) for head in picked]
        cums, shrunk, carry, steps = state_terms(
            [k_ref[:, span] for span in spans],
            [v_ref[:, span] for span in spans],
            [d_ref[:, span] for span in spans],
            [r_ref[pl.ds(head, 1), :] for head in picked],
        )
        for head, cum, shrink, carried in zip(picked, cums, shrunk, carry):
            kept_cum[head] = cum
            kept_key[head] = shrink
            kept_carry[head] = carried
        return places_in, steps

    def outputs(turn, whose):
        picked = [
            owner * per + index for owner in turn_owners(turn, whose) for index in range(per)
        ]
        results = output_terms(
            [q_ref[:, columns(head)] for head in picked],
            [kept_cum[head] for head in picked],
            [kept_key[head] for head in picked],
            [kept_carry[head] for head in picked],
            [r_ref[pl.ds(head, 1), :] for head in picked],
        )
        for head, (head_reach, head_local) in zip(picked, results):
            reach[head] = head_reach
            local[head] = head_local

    def mate_copy(spot, slot):
        return pltpu.make_async_remote_copy(
            src_ref=outgo.at[spot],
            dst_ref=duo.at[spot, slot],
            send_sem=mate_send.at[spot],
            recv_sem=mate_recv.at[spot],
            device_id=(grp, mate),
            device_id_type=MESH,
        )

    def up_copy(spot, shard, host):
        return pltpu.make_async_remote_copy(
            src_ref=comp.at[spot],
            dst_ref=arrived.at[shard, lax.rem(spot, per)],
            send_sem=up_send.at[spot],
            recv_sem=up_recv.at[shard, lax.rem(spot, per)],
            device_id=(grp, 2 * host + side),
            device_id_type=MESH,
        )

    def for_mate(turn, _):
        spots, steps = compute(turn, 1 - side)
        for spot, step in zip(spots, steps):
            outgo[spot] = step
            mate_copy(spot, side).start()
        return 0

    lax.fori_loop(0, turns, for_mate, 0)

    def for_pair(turn, _):
        spots, steps = compute(turn, side)
        for spot, step in zip(spots, steps):
            duo[spot, side] = step
        for spot in spots:
            mate_copy(spot, 1 - side).wait_recv()
        joined = [join(duo[spot, 1], duo[spot, 0]) for spot in spots]
        for spot, (whole, added) in zip(spots, joined):
            comp[spot, :, :size] = whole
            comp[spot, :, size:] = added
            host = lax.div(spot, per)

            @pl.when(host != place)
            def _():
                up_copy(spot, place, host).start()

            @pl.when(host == place)
            def _():
                arrived[place, lax.rem(spot, per)] = comp[spot]

        outputs(turn, 1 - side)
        return 0

    query_copy.wait()
    lax.fori_loop(0, turns, for_pair, 0)

    rows = lax.broadcasted_iota(jnp.int32, (size, 2 * size), 0)
    cols = lax.broadcasted_iota(jnp.int32, (size, 2 * size), 1)

    def total_copy(target):
        return pltpu.make_async_remote_copy(
            src_ref=prior.at[places],
            dst_ref=total_in,
            send_sem=total_send,
            recv_sem=total_recv,
            device_id=(target, me),
            device_id_type=MESH,
        )

    def pair_copy(ahead):
        return pltpu.make_async_remote_copy(
            src_ref=onward,
            dst_ref=pair_in,
            send_sem=pair_send.at[ahead - 1],
            recv_sem=pair_recv,
            device_id=(grp + ahead, me),
            device_id_type=MESH,
        )

    def down_copy(shard, host):
        return pltpu.make_async_remote_copy(
            src_ref=starts.at[shard],
            dst_ref=slots.at[0, pl.ds(host * per, per)],
            send_sem=down_send.at[shard],
            recv_sem=down_recv.at[host],
            device_id=(grp, 2 * shard + side),
            device_id_type=MESH,
        )

    def relay_copy(host):
        return pltpu.make_async_remote_copy(
            src_ref=slots.at[1 - side, pl.ds(host * per, per)],
            dst_ref=begin.at[pl.ds(host * per, per)],
            send_sem=relay_send.at[host],
            recv_sem=relay_recv.at[host],
            device_id=(grp, mate),
            device_id_type=MESH,
        )

    def compose():
        for index in range(per):
            prior[0, index] = jnp.where(rows == cols, 1.0, 0.0).astype(F32)

        def advance(shard, _):
            @pl.when(shard != place)
            def _():
                for index in range(per):
                    up_copy(place * per + index, shard, place).wait_recv()

            for index in range(per):
                whole, added = join(arrived[shard, index], prior[shard, index])
                prior[shard + 1, index, :, :size] = whole
                prior[shard + 1, index, :, size:] = added
            return 0

        lax.fori_loop(0, places, advance, 0)

        @pl.when(odd == 0)
        def _():
            total_copy(grp + 1).start()

        @pl.when(pair == 0)
        def _():
            pair_in[...] = jnp.zeros_like(pair_in)

        @pl.when(odd == 1)
        def _():
            total_copy(grp).wait_recv()
            both = [join(prior[places, index], total_in[index]) for index in range(per)]

            @pl.when(pair > 0)
            def _():
                pair_copy(1).wait_recv()

            for index in range(per):
                onward[index] = mul(both[index][0], pair_in[index]) + both[index][1]

            @pl.when(pair < last_pair)
            def _():
                pair_copy(2).start()
                pair_copy(1).start()

            for index in range(per):
                entry[index] = apply(total_in[index], pair_in[index])

        @pl.when(odd == 0)
        def _():
            @pl.when(pair > 0)
            def _():
                pair_copy(1).wait_recv()

            entry[...] = pair_in[...]

        def give(step, _):
            shard = far_first(step, place, places)
            for index in range(per):
                starts[shard, index] = apply(prior[shard, index], entry[index])

            @pl.when(shard != place)
            def _():
                down_copy(shard, place).start()

            @pl.when(shard == place)
            def _():
                slots[0, pl.ds(place * per, per)] = starts[shard]

            return 0

        lax.fori_loop(0, places, give, 0)

    when_owner(compose)

    def own_outputs(turn, _):
        outputs(turn, side)
        return 0

    lax.fori_loop(0, turns, own_outputs, 0)
    gate_copy.wait()

    def finish(owner, states):
        for index in range(per):
            head = owner * per + index
            raw = mul(reach[head], states[index]) + local[head]
            scaled = raw * lax.rsqrt(jnp.mean(raw * raw, axis=-1, keepdims=True) + 1e-05)
            gate = g_ref[:, columns(head)].astype(F32)
            o_ref[:, columns(head)] = (scaled / (1.0 + jnp.exp(-gate))).astype(BF16)

    def nearest(step):
        return near_first(step, place, hosts) if everyone else step

    def relay(step, _):
        host = nearest(step)

        @pl.when(host != place)
        def _():
            down_copy(place, host).wait_recv()

        for index in range(per):
            spot = host * per + index
            slots[1, spot] = apply(duo[spot, 0], slots[0, spot])
        relay_copy(host).start()
        finish(2 * host + side, [slots[side, host * per + index] for index in range(per)])
        return 0

    lax.fori_loop(0, hosts, relay, 0)

    def last(step, _):
        host = nearest(step)
        relay_copy(host).wait_recv()
        finish(2 * host + 1 - side, [begin[host * per + index] for index in range(per)])
        return 0

    lax.fori_loop(0, hosts, last, 0)

    def drain(spot, _):
        mate_copy(spot, side).wait_send()
        host = lax.div(spot, per)

        @pl.when(host != place)
        def _():
            up_copy(spot, place, host).wait_send()

        return 0

    lax.fori_loop(0, heads // 2, drain, 0)

    def drain_down():
        @pl.when(odd == 0)
        def _():
            total_copy(grp + 1).wait_send()

        @pl.when(jnp.logical_and(odd == 1, pair < last_pair))
        def _():
            pair_copy(2).wait_send()
            pair_copy(1).wait_send()

        def one(shard, _):
            @pl.when(shard != place)
            def _():
                down_copy(shard, place).wait_send()

            return 0

        lax.fori_loop(0, places, one, 0)

    when_owner(drain_down)

    def drain_relay(host, _):
        relay_copy(host).wait_send()
        return 0

    lax.fori_loop(0, hosts, drain_relay, 0)


def shards(groups, count, queries, key_vectors, values, log_decay, write_rate, out_gate):
    seq_count, local_len, features = queries.shape
    heads = write_rate.shape[1]
    size = features // heads
    per = max(heads // count, 1)
    owners = heads // per
    half, places, hosts = heads // 2, count // 2, owners // 2
    dma = pltpu.SemaphoreType.DMA
    square = (size, size)
    wide = (size, 2 * size)
    call = pl.pallas_call(
        functools.partial(kernel, groups, count, heads),
        out_shape=jax.ShapeDtypeStruct((local_len, features), BF16),
        in_specs=[pl.BlockSpec(memory_space=pltpu.HBM)] * 5
        + [pl.BlockSpec(memory_space=pltpu.VMEM)],
        out_specs=pl.BlockSpec(memory_space=pltpu.VMEM),
        scratch_shapes=[pltpu.VMEM((local_len, features), BF16)] * 5
        + [
            pltpu.VMEM((half, *wide), F32),
            pltpu.VMEM((half, 2, *wide), F32),
            pltpu.VMEM((half, *wide), F32),
            pltpu.VMEM((places, per, *wide), F32),
            pltpu.VMEM((places + 1, per, *wide), F32),
            pltpu.VMEM((per, *wide), F32),
            pltpu.VMEM((per, *square), F32),
            pltpu.VMEM((per, *square), F32),
            pltpu.VMEM((per, *square), F32),
            pltpu.VMEM((places, per, *square), F32),
            pltpu.VMEM((2, half, *square), F32),
            pltpu.VMEM((half, *square), F32),
            pltpu.VMEM((heads, local_len, size), F32),
            pltpu.VMEM((heads, local_len, size), F32),
            pltpu.VMEM((heads, local_len, size), F32),
            pltpu.VMEM((heads, local_len, size), F32),
            pltpu.VMEM((heads, local_len, 2 * size), F32),
            dma((3, owners)),
            dma,
            dma,
            dma((half,)),
            dma((half,)),
            dma((half,)),
            dma((places, per)),
            dma,
            dma,
            dma((2,)),
            dma,
            dma((places,)),
            dma((hosts,)),
            dma((hosts,)),
            dma((hosts,)),
        ],
        compiler_params=pltpu.CompilerParams(
            collective_id=0, has_side_effects=True, vmem_limit_bytes=63 * 1024 * 1024
        ),
        name="delta_attention",
    )
    result = call(
        queries[0], key_vectors[0], values[0], log_decay[0], out_gate[0], write_rate[0]
    )
    return result[None]


def solution(mesh):
    spread = P(None, ("grp", "seq"), None)
    return jax.shard_map(
        functools.partial(shards, mesh.shape["grp"], mesh.shape["seq"]),
        mesh=mesh,
        in_specs=(spread, spread, spread, spread, P(None, None, ("grp", "seq")), spread),
        out_specs=spread,
        check_vma=False,
    )
```

```python
import functools
import jax
import jax.numpy as jnp
from jax import lax
from jax.experimental import pallas as pl
from jax.experimental.pallas import tpu as pltpu
from jax.sharding import PartitionSpec as P

BLOCK = 64
BATCH = 2
MESH = pl.DeviceIdType.MESH
F32 = jnp.float32
BF16 = jnp.bfloat16


def split(value):
    high = value.astype(BF16)
    return high, (value - high.astype(F32)).astype(BF16)


def mul(left, right):
    width = right.shape[1]
    lhs = jnp.concatenate(split(left), axis=1)
    parts = jnp.concatenate(split(right), axis=1)
    out = jnp.dot(lhs, jnp.concatenate([parts, parts], axis=0), preferred_element_type=F32)
    return out[:, :width] + out[:, width:]


def mul_split(left, right):
    width = right[0].shape[1]
    parts = jnp.concatenate(right, axis=1)
    out = jnp.dot(
        jnp.concatenate(left, axis=1),
        jnp.concatenate([parts, parts], axis=0),
        preferred_element_type=F32,
    )
    return out[:, :width] + out[:, width:]


def mul_rows(left, right):
    width = right.shape[0]
    lhs = jnp.concatenate(split(left), axis=1)
    parts = jnp.concatenate(split(right), axis=0)
    rhs = jnp.concatenate([parts, parts], axis=1)
    out = lax.dot_general(lhs, rhs, (((1,), (1,)), ((), ())), preferred_element_type=F32)
    return out[:, :width] + out[:, width:]


def mul_wide(left, right):
    high, low = split(left)
    r_high, r_low = split(right)
    lhs = jnp.concatenate([high, low], axis=1)
    rhs = jnp.concatenate([r_high, r_high], axis=0)
    return jnp.dot(lhs, rhs, preferred_element_type=F32) + jnp.dot(
        high, r_low, preferred_element_type=F32
    )


def mul_both(upper, lower, right):
    width = right[0].shape[1]
    lhs = jnp.concatenate(
        [jnp.concatenate([up, low], axis=0) for up, low in zip(upper, lower)], axis=1
    )
    parts = jnp.concatenate(right, axis=1)
    out = jnp.dot(lhs, jnp.concatenate([parts, parts], axis=0), preferred_element_type=F32)
    return out[:, :width] + out[:, width:]


def state_terms(keys, values, decays, rates):
    extent, size = keys[0].shape
    half = extent // 2
    rows = lax.broadcasted_iota(jnp.int32, (extent, extent), 0)
    cols = lax.broadcasted_iota(jnp.int32, (extent, extent), 1)
    same = (rows >= half) == (cols >= half)
    eye = jnp.where(rows == cols, 1.0, 0.0).astype(F32)
    ones = jnp.where(rows >= cols, 1.0, 0.0).astype(BF16)
    cums = [jnp.dot(ones, decay, preferred_element_type=F32) for decay in decays]
    units = []
    for key in keys:
        key_f = key.astype(F32)
        units.append(key_f * lax.rsqrt(jnp.sum(key_f * key_f, axis=-1, keepdims=True) + 1e-06))
    shrunk = [unit * jnp.exp(cum[half - 1 : half] - cum) for unit, cum in zip(units, cums)]
    pairs = [
        mul_rows(unit * jnp.exp(cum - cum[half - 1 : half]), shrink)
        for unit, cum, shrink in zip(units, cums, shrunk)
    ]
    lowers = [jnp.where(rows > cols, product * rate, 0.0) for product, rate in zip(pairs, rates)]
    diag = [jnp.where(same, lower, 0.0) for lower in lowers]
    below = [jnp.where(same, 0.0, lower) for lower in lowers]
    inverse = [eye - part for part in diag]
    power = [split(mul(part, part)) for part in diag]
    for _ in range(half.bit_length() - 3):
        both = [mul_both(split(x), p, p) for x, p in zip(inverse, power)]
        inverse = [x + b[:extent] for x, b in zip(inverse, both)]
        power = [split(b[extent:]) for b in both]
    inverse = [x + mul_split(split(x), p) for x, p in zip(inverse, power)]
    corner = [mul(x[half:], c) for x, c in zip(inverse, below)]
    corner = [mul(c, x) for c, x in zip(corner, inverse)]
    inverse = [
        jnp.concatenate([x[:half], x[half:] - c], axis=0) for x, c in zip(inverse, corner)
    ]
    carry = [
        mul_wide(x, jnp.concatenate([unit * jnp.exp(cum), value.astype(F32)], axis=1))
        for x, unit, cum, value in zip(inverse, units, cums, values)
    ]
    steps = []
    for unit, cum, rate, carried in zip(units, cums, rates, carry):
        last = cum[extent - 1 : extent]
        key_end = jnp.transpose(unit * jnp.exp(last - cum)) * rate
        out = mul_wide(key_end, carried)
        step_map = jnp.where(rows == cols, jnp.exp(last), 0.0) - out[:, :size]
        steps.append(jnp.concatenate([step_map, out[:, size:]], axis=1))
    return cums, shrunk, carry, steps


def output_terms(queries, cums, shrunk, carry, rates):
    extent, size = queries[0].shape
    half = extent // 2
    rows = lax.broadcasted_iota(jnp.int32, (extent, extent), 0)
    cols = lax.broadcasted_iota(jnp.int32, (extent, extent), 1)
    q_f = [query.astype(F32) for query in queries]
    pairs = [
        mul_rows(query * jnp.exp(cum - cum[half - 1 : half]), shrink)
        for query, cum, shrink in zip(q_f, cums, shrunk)
    ]
    attends = [jnp.where(rows >= cols, product * rate, 0.0) for product, rate in zip(pairs, rates)]
    outs = [mul_wide(attend, carried) for attend, carried in zip(attends, carry)]
    return [
        (query * jnp.exp(cum) - out[:, :size], out[:, size:])
        for query, cum, out in zip(q_f, cums, outs)
    ]


def flip(own, high, low):
    return 2 * lax.rem(lax.div(own, 2) + high, 2) + lax.rem(lax.rem(own, 2) + low, 2)


def far_first(step, own, extent):
    if extent != 4:
        return lax.rem(own + 1 + step, extent)
    late = lax.div(step, 2)
    return flip(own, 1 - late, lax.rem(step + late, 2))


def near_first(step, own, extent):
    if extent != 4:
        return lax.rem(own + extent - step, extent)
    return flip(own, lax.div(step, 2), lax.rem(step, 2))


def kernel(
    groups, count, heads,
    q_hbm, k_hbm, v_hbm, d_hbm, g_hbm, r_ref, o_ref,
    q_ref, k_ref, v_ref, d_ref, g_ref,
    outgo, duo, comp, arrived, prior, total_in, pair_in, entry, onward, starts, slots, begin,
    reach, local, kept_cum, kept_key, kept_carry,
    load_sem, query_sem, gate_sem, mate_send, mate_recv, up_send, up_recv,
    total_send, total_recv, pair_send, pair_recv, down_send, down_recv, relay_send, relay_recv,
):
    grp, me = lax.axis_index("grp"), lax.axis_index("seq")
    per = max(heads // count, 1)
    owners = heads // per
    size = q_ref.shape[1] // heads
    everyone = owners == count
    places, hosts = count // 2, owners // 2
    place, side = lax.div(me, 2), lax.rem(me, 2)
    mate = me + 1 - 2 * side
    turns = heads // 2 // BATCH
    runs = BATCH // per
    own_turn = lax.rem(lax.div(per * place, BATCH), turns)
    pair, odd = lax.div(grp, 2), lax.rem(grp, 2)
    last_pair = groups // 2 - 1

    def when_owner(body):
        if everyone:
            body()
        else:
            pl.when(me < owners)(body)

    def greet_at(group, seq):
        pl.semaphore_signal(barrier, inc=1, device_id=(group, seq), device_id_type=MESH)

    barrier = pltpu.get_barrier_semaphore()
    greet_at(grp, mate)

    def greet(step, _):
        greet_at(grp, lax.rem(me + 2 * step, count))
        return 0

    lax.fori_loop(1, places, greet, 0)

    @pl.when(odd == 0)
    def _():
        greet_at(grp + 1, me)

    @pl.when(odd == 1)
    def _():
        greet_at(grp - 1, me)

    @pl.when(jnp.logical_and(odd == 0, pair > 0))
    def _():
        greet_at(grp - 1, me)

    @pl.when(jnp.logical_and(odd == 1, pair > 0))
    def _():
        greet_at(grp - 2, me)

    @pl.when(jnp.logical_and(odd == 1, pair < last_pair))
    def _():
        greet_at(grp + 1, me)
        greet_at(grp + 2, me)

    def turn_owners(turn, whose):
        start = far_first(jnp.int32(turn), own_turn, turns) * runs
        return [2 * (start + run) + whose for run in range(runs)]

    def owner_columns(owner):
        return pl.ds(pl.multiple_of(owner * (per * size), per * size), per * size)

    def load(owner):
        span = owner_columns(owner)
        return [
            pltpu.make_async_copy(far.at[:, span], near.at[:, span], load_sem.at[index, owner])
            for index, (far, near) in enumerate(
                [(d_hbm, d_ref), (k_hbm, k_ref), (v_hbm, v_ref)]
            )
        ]

    for turn in range(turns):
        for whose in (1 - side, side):
            for owner in turn_owners(turn, whose):
                for copy in load(owner):
                    copy.start()
    query_copy = pltpu.make_async_copy(q_hbm, q_ref, query_sem)
    query_copy.start()
    gate_copy = pltpu.make_async_copy(g_hbm, g_ref, gate_sem)
    gate_copy.start()

    beside = 1 + jnp.minimum(pair, 1) + 2 * odd * jnp.minimum(last_pair - pair, 1)
    pl.semaphore_wait(barrier, places + beside)

    def columns(head):
        return pl.ds(pl.multiple_of(head * size, size), size)

    def join(late, early):
        product = mul_wide(late[:, :size], early)
        return product[:, :size], product[:, size:] + late[:, size:]

    def apply(step, state):
        return mul(step[:, :size], state) + step[:, size:]

    def turn_spots(turn):
        return [
            lax.div(owner, 2) * per + index
            for owner in turn_owners(turn, side)
            for index in range(per)
        ]

    def compute(turn):
        turn_of = turn_owners(turn, 1 - side) + turn_owners(turn, side)
        for owner in turn_of:
            for copy in load(owner):
                copy.wait()
        picked = [owner * per + index for owner in turn_of for index in range(per)]
        spans = [columns(head) for head in picked]
        cums, shrunk, carry, steps = state_terms(
            [k_ref[:, span] for span in spans],
            [v_ref[:, span] for span in spans],
            [d_ref[:, span] for span in spans],
            [r_ref[pl.ds(head, 1), :] for head in picked],
        )
        for head, cum, shrink, carried in zip(picked, cums, shrunk, carry):
            kept_cum[head] = cum
            kept_key[head] = shrink
            kept_carry[head] = carried
        return steps

    def outputs(turn, whose):
        picked = [
            owner * per + index for owner in turn_owners(turn, whose) for index in range(per)
        ]
        results = output_terms(
            [q_ref[:, columns(head)] for head in picked],
            [kept_cum[head] for head in picked],
            [kept_key[head] for head in picked],
            [kept_carry[head] for head in picked],
            [r_ref[pl.ds(head, 1), :] for head in picked],
        )
        for head, (head_reach, head_local) in zip(picked, results):
            reach[head] = head_reach
            local[head] = head_local

    def mate_copy(spot, slot):
        return pltpu.make_async_remote_copy(
            src_ref=outgo.at[spot],
            dst_ref=duo.at[spot, slot],
            send_sem=mate_send.at[spot],
            recv_sem=mate_recv.at[spot],
            device_id=(grp, mate),
            device_id_type=MESH,
        )

    def up_copy(spot, shard, host):
        return pltpu.make_async_remote_copy(
            src_ref=comp.at[spot],
            dst_ref=arrived.at[shard, lax.rem(spot, per)],
            send_sem=up_send.at[spot],
            recv_sem=up_recv.at[shard, lax.rem(spot, per)],
            device_id=(grp, 2 * host + side),
            device_id_type=MESH,
        )

    def pair_up(turn):
        spots = turn_spots(turn)
        for spot in spots:
            mate_copy(spot, 1 - side).wait_recv()
        joined = [join(duo[spot, 1], duo[spot, 0]) for spot in spots]
        for spot, (whole, added) in zip(spots, joined):
            comp[spot, :, :size] = whole
            comp[spot, :, size:] = added
            host = lax.div(spot, per)

            @pl.when(host != place)
            def _():
                up_copy(spot, place, host).start()

            @pl.when(host == place)
            def _():
                arrived[place, lax.rem(spot, per)] = comp[spot]

    def first_phase(turn, _):
        spots = turn_spots(turn)
        steps = compute(turn)
        for spot, step in zip(spots, steps[:BATCH]):
            outgo[spot] = step
            mate_copy(spot, side).start()
        for spot, step in zip(spots, steps[BATCH:]):
            duo[spot, side] = step

        @pl.when(turn > 0)
        def _():
            pair_up(turn - 1)

        return 0

    lax.fori_loop(0, turns, first_phase, 0)
    pair_up(turns - 1)
    query_copy.wait()

    rows = lax.broadcasted_iota(jnp.int32, (size, 2 * size), 0)
    cols = lax.broadcasted_iota(jnp.int32, (size, 2 * size), 1)

    def total_copy(target):
        return pltpu.make_async_remote_copy(
            src_ref=prior.at[places],
            dst_ref=total_in,
            send_sem=total_send,
            recv_sem=total_recv,
            device_id=(target, me),
            device_id_type=MESH,
        )

    def pair_copy(ahead):
        return pltpu.make_async_remote_copy(
            src_ref=onward,
            dst_ref=pair_in,
            send_sem=pair_send.at[ahead - 1],
            recv_sem=pair_recv,
            device_id=(grp + ahead, me),
            device_id_type=MESH,
        )

    def down_copy(shard, host):
        return pltpu.make_async_remote_copy(
            src_ref=starts.at[shard],
            dst_ref=slots.at[0, pl.ds(host * per, per)],
            send_sem=down_send.at[shard],
            recv_sem=down_recv.at[host],
            device_id=(grp, 2 * shard + side),
            device_id_type=MESH,
        )

    def relay_copy(host):
        return pltpu.make_async_remote_copy(
            src_ref=slots.at[1 - side, pl.ds(host * per, per)],
            dst_ref=begin.at[pl.ds(host * per, per)],
            send_sem=relay_send.at[host],
            recv_sem=relay_recv.at[host],
            device_id=(grp, mate),
            device_id_type=MESH,
        )

    def compose():
        for index in range(per):
            prior[0, index] = jnp.where(rows == cols, 1.0, 0.0).astype(F32)

        def advance(shard, _):
            @pl.when(shard != place)
            def _():
                for index in range(per):
                    up_copy(place * per + index, shard, place).wait_recv()

            for index in range(per):
                whole, added = join(arrived[shard, index], prior[shard, index])
                prior[shard + 1, index, :, :size] = whole
                prior[shard + 1, index, :, size:] = added
            return 0

        lax.fori_loop(0, places, advance, 0)

        @pl.when(odd == 0)
        def _():
            total_copy(grp + 1).start()

        @pl.when(pair == 0)
        def _():
            pair_in[...] = jnp.zeros_like(pair_in)

        @pl.when(odd == 1)
        def _():
            total_copy(grp).wait_recv()
            both = [join(prior[places, index], total_in[index]) for index in range(per)]

            @pl.when(pair > 0)
            def _():
                pair_copy(1).wait_recv()

            for index in range(per):
                onward[index] = mul(both[index][0], pair_in[index]) + both[index][1]

            @pl.when(pair < last_pair)
            def _():
                pair_copy(2).start()
                pair_copy(1).start()

            for index in range(per):
                entry[index] = apply(total_in[index], pair_in[index])

        @pl.when(odd == 0)
        def _():
            @pl.when(pair > 0)
            def _():
                pair_copy(1).wait_recv()

            entry[...] = pair_in[...]

        def give(step, _):
            shard = far_first(step, place, places)
            for index in range(per):
                starts[shard, index] = apply(prior[shard, index], entry[index])

            @pl.when(shard != place)
            def _():
                down_copy(shard, place).start()

            @pl.when(shard == place)
            def _():
                slots[0, pl.ds(place * per, per)] = starts[shard]

            return 0

        lax.fori_loop(0, places, give, 0)

    when_owner(compose)

    def own_outputs(turn, _):
        outputs(turn, side)
        return 0

    lax.fori_loop(0, turns, own_outputs, 0)
    gate_copy.wait()

    def finish(owner, states):
        for index in range(per):
            head = owner * per + index
            raw = mul(reach[head], states[index]) + local[head]
            scaled = raw * lax.rsqrt(jnp.mean(raw * raw, axis=-1, keepdims=True) + 1e-05)
            gate = g_ref[:, columns(head)].astype(F32)
            o_ref[:, columns(head)] = (scaled / (1.0 + jnp.exp(-gate))).astype(BF16)

    def nearest(step):
        return near_first(step, place, hosts) if everyone else step

    def relay(step, _):
        host = nearest(step)

        @pl.when(step < turns)
        def _():
            outputs(step, 1 - side)

        @pl.when(host != place)
        def _():
            down_copy(place, host).wait_recv()

        for index in range(per):
            spot = host * per + index
            slots[1, spot] = apply(duo[spot, 0], slots[0, spot])
        relay_copy(host).start()
        finish(2 * host + side, [slots[side, host * per + index] for index in range(per)])
        return 0

    lax.fori_loop(0, hosts, relay, 0)

    def last(step, _):
        host = nearest(step)
        relay_copy(host).wait_recv()
        finish(2 * host + 1 - side, [begin[host * per + index] for index in range(per)])
        return 0

    lax.fori_loop(0, hosts, last, 0)

    def drain(spot, _):
        mate_copy(spot, side).wait_send()
        host = lax.div(spot, per)

        @pl.when(host != place)
        def _():
            up_copy(spot, place, host).wait_send()

        return 0

    lax.fori_loop(0, heads // 2, drain, 0)

    def drain_down():
        @pl.when(odd == 0)
        def _():
            total_copy(grp + 1).wait_send()

        @pl.when(jnp.logical_and(odd == 1, pair < last_pair))
        def _():
            pair_copy(2).wait_send()
            pair_copy(1).wait_send()

        def one(shard, _):
            @pl.when(shard != place)
            def _():
                down_copy(shard, place).wait_send()

            return 0

        lax.fori_loop(0, places, one, 0)

    when_owner(drain_down)

    def drain_relay(host, _):
        relay_copy(host).wait_send()
        return 0

    lax.fori_loop(0, hosts, drain_relay, 0)


def shards(groups, count, queries, key_vectors, values, log_decay, write_rate, out_gate):
    seq_count, local_len, features = queries.shape
    heads = write_rate.shape[1]
    size = features // heads
    per = max(heads // count, 1)
    owners = heads // per
    half, places, hosts = heads // 2, count // 2, owners // 2
    dma = pltpu.SemaphoreType.DMA
    square = (size, size)
    wide = (size, 2 * size)
    call = pl.pallas_call(
        functools.partial(kernel, groups, count, heads),
        out_shape=jax.ShapeDtypeStruct((local_len, features), BF16),
        in_specs=[pl.BlockSpec(memory_space=pltpu.HBM)] * 5
        + [pl.BlockSpec(memory_space=pltpu.VMEM)],
        out_specs=pl.BlockSpec(memory_space=pltpu.VMEM),
        scratch_shapes=[pltpu.VMEM((local_len, features), BF16)] * 5
        + [
            pltpu.VMEM((half, *wide), F32),
            pltpu.VMEM((half, 2, *wide), F32),
            pltpu.VMEM((half, *wide), F32),
            pltpu.VMEM((places, per, *wide), F32),
            pltpu.VMEM((places + 1, per, *wide), F32),
            pltpu.VMEM((per, *wide), F32),
            pltpu.VMEM((per, *square), F32),
            pltpu.VMEM((per, *square), F32),
            pltpu.VMEM((per, *square), F32),
            pltpu.VMEM((places, per, *square), F32),
            pltpu.VMEM((2, half, *square), F32),
            pltpu.VMEM((half, *square), F32),
            pltpu.VMEM((heads, local_len, size), F32),
            pltpu.VMEM((heads, local_len, size), F32),
            pltpu.VMEM((heads, local_len, size), F32),
            pltpu.VMEM((heads, local_len, size), F32),
            pltpu.VMEM((heads, local_len, 2 * size), F32),
            dma((3, owners)),
            dma,
            dma,
            dma((half,)),
            dma((half,)),
            dma((half,)),
            dma((places, per)),
            dma,
            dma,
            dma((2,)),
            dma,
            dma((places,)),
            dma((hosts,)),
            dma((hosts,)),
            dma((hosts,)),
        ],
        compiler_params=pltpu.CompilerParams(
            collective_id=0, has_side_effects=True, vmem_limit_bytes=63 * 1024 * 1024
        ),
        name="delta_attention",
    )
    result = call(
        queries[0], key_vectors[0], values[0], log_decay[0], out_gate[0], write_rate[0]
    )
    return result[None]


def solution(mesh):
    spread = P(None, ("grp", "seq"), None)
    return jax.shard_map(
        functools.partial(shards, mesh.shape["grp"], mesh.shape["seq"]),
        mesh=mesh,
        in_specs=(spread, spread, spread, spread, P(None, None, ("grp", "seq")), spread),
        out_specs=spread,
        check_vma=False,
    )
```

```python
import functools
import jax
import jax.numpy as jnp
from jax import lax
from jax.experimental import pallas as pl
from jax.experimental.pallas import tpu as pltpu
from jax.sharding import PartitionSpec as P

BLOCK = 64
BATCH = 2
MESH = pl.DeviceIdType.MESH
F32 = jnp.float32
BF16 = jnp.bfloat16


def split(value):
    high = value.astype(BF16)
    return high, (value - high.astype(F32)).astype(BF16)


def mul(left, right):
    width = right.shape[1]
    lhs = jnp.concatenate(split(left), axis=1)
    parts = jnp.concatenate(split(right), axis=1)
    out = jnp.dot(lhs, jnp.concatenate([parts, parts], axis=0), preferred_element_type=F32)
    return out[:, :width] + out[:, width:]


def mul_split(left, right):
    width = right[0].shape[1]
    parts = jnp.concatenate(right, axis=1)
    out = jnp.dot(
        jnp.concatenate(left, axis=1),
        jnp.concatenate([parts, parts], axis=0),
        preferred_element_type=F32,
    )
    return out[:, :width] + out[:, width:]


def mul_rows(left, right):
    width = right.shape[0]
    lhs = jnp.concatenate(split(left), axis=1)
    parts = jnp.concatenate(split(right), axis=0)
    rhs = jnp.concatenate([parts, parts], axis=1)
    out = lax.dot_general(lhs, rhs, (((1,), (1,)), ((), ())), preferred_element_type=F32)
    return out[:, :width] + out[:, width:]


def mul_wide(left, right):
    high, low = split(left)
    r_high, r_low = split(right)
    lhs = jnp.concatenate([high, low], axis=1)
    rhs = jnp.concatenate([r_high, r_high], axis=0)
    return jnp.dot(lhs, rhs, preferred_element_type=F32) + jnp.dot(
        high, r_low, preferred_element_type=F32
    )


def mul_both(upper, lower, right):
    width = right[0].shape[1]
    lhs = jnp.concatenate(
        [jnp.concatenate([up, low], axis=0) for up, low in zip(upper, lower)], axis=1
    )
    parts = jnp.concatenate(right, axis=1)
    out = jnp.dot(lhs, jnp.concatenate([parts, parts], axis=0), preferred_element_type=F32)
    return out[:, :width] + out[:, width:]


def state_terms(keys, values, decays, rates):
    extent, size = keys[0].shape
    half = extent // 2
    rows = lax.broadcasted_iota(jnp.int32, (extent, extent), 0)
    cols = lax.broadcasted_iota(jnp.int32, (extent, extent), 1)
    same = (rows >= half) == (cols >= half)
    eye = jnp.where(rows == cols, 1.0, 0.0).astype(F32)
    ones = jnp.where(rows >= cols, 1.0, 0.0).astype(BF16)
    cums = [jnp.dot(ones, decay, preferred_element_type=F32) for decay in decays]
    units = []
    for key in keys:
        key_f = key.astype(F32)
        units.append(key_f * lax.rsqrt(jnp.sum(key_f * key_f, axis=-1, keepdims=True) + 1e-06))
    shrunk = [unit * jnp.exp(cum[half - 1 : half] - cum) for unit, cum in zip(units, cums)]
    pairs = [
        mul_rows(unit * jnp.exp(cum - cum[half - 1 : half]), shrink)
        for unit, cum, shrink in zip(units, cums, shrunk)
    ]
    lowers = [jnp.where(rows > cols, product * rate, 0.0) for product, rate in zip(pairs, rates)]
    diag = [jnp.where(same, lower, 0.0) for lower in lowers]
    below = [jnp.where(same, 0.0, lower) for lower in lowers]
    inverse = [eye - part for part in diag]
    power = [split(mul(part, part)) for part in diag]
    for _ in range(half.bit_length() - 3):
        both = [mul_both(split(x), p, p) for x, p in zip(inverse, power)]
        inverse = [x + b[:extent] for x, b in zip(inverse, both)]
        power = [split(b[extent:]) for b in both]
    inverse = [x + mul_split(split(x), p) for x, p in zip(inverse, power)]
    corner = [mul(x[half:], c) for x, c in zip(inverse, below)]
    corner = [mul(c, x) for c, x in zip(corner, inverse)]
    inverse = [
        jnp.concatenate([x[:half], x[half:] - c], axis=0) for x, c in zip(inverse, corner)
    ]
    carry = [
        mul_wide(x, jnp.concatenate([unit * jnp.exp(cum), value.astype(F32)], axis=1))
        for x, unit, cum, value in zip(inverse, units, cums, values)
    ]
    steps = []
    for unit, cum, rate, carried in zip(units, cums, rates, carry):
        last = cum[extent - 1 : extent]
        key_end = jnp.transpose(unit * jnp.exp(last - cum)) * rate
        out = mul_wide(key_end, carried)
        step_map = jnp.where(rows == cols, jnp.exp(last), 0.0) - out[:, :size]
        steps.append(jnp.concatenate([step_map, out[:, size:]], axis=1))
    return cums, shrunk, carry, steps


def output_terms(queries, cums, shrunk, carry, rates):
    extent, size = queries[0].shape
    half = extent // 2
    rows = lax.broadcasted_iota(jnp.int32, (extent, extent), 0)
    cols = lax.broadcasted_iota(jnp.int32, (extent, extent), 1)
    q_f = [query.astype(F32) for query in queries]
    pairs = [
        mul_rows(query * jnp.exp(cum - cum[half - 1 : half]), shrink)
        for query, cum, shrink in zip(q_f, cums, shrunk)
    ]
    attends = [jnp.where(rows >= cols, product * rate, 0.0) for product, rate in zip(pairs, rates)]
    outs = [mul_wide(attend, carried) for attend, carried in zip(attends, carry)]
    return [
        (query * jnp.exp(cum) - out[:, :size], out[:, size:])
        for query, cum, out in zip(q_f, cums, outs)
    ]


def flip(own, high, low):
    return 2 * lax.rem(lax.div(own, 2) + high, 2) + lax.rem(lax.rem(own, 2) + low, 2)


def far_first(step, own, extent):
    if extent != 4:
        return lax.rem(own + 1 + step, extent)
    late = lax.div(step, 2)
    return flip(own, 1 - late, lax.rem(step + late, 2))


def near_first(step, own, extent):
    if extent != 4:
        return lax.rem(own + extent - step, extent)
    return flip(own, lax.div(step, 2), lax.rem(step, 2))


def kernel(
    groups, count, heads,
    q_hbm, k_hbm, v_hbm, d_hbm, g_hbm, r_ref, o_ref,
    q_ref, k_ref, v_ref, d_ref, g_ref,
    outgo, duo, comp, arrived, prior, total_in, pair_in, entry, onward, starts, slots, begin,
    reach, local, kept_cum, kept_key, kept_carry,
    load_sem, query_sem, gate_sem, mate_send, mate_recv, up_send, up_recv,
    total_send, total_recv, pair_send, pair_recv, down_send, down_recv, relay_send, relay_recv,
):
    grp, me = lax.axis_index("grp"), lax.axis_index("seq")
    per = max(heads // count, 1)
    owners = heads // per
    size = q_ref.shape[1] // heads
    everyone = owners == count
    places, hosts = count // 2, owners // 2
    place, side = lax.div(me, 2), lax.rem(me, 2)
    mate = me + 1 - 2 * side
    turns = heads // 2 // BATCH
    runs = BATCH // per
    own_turn = lax.rem(lax.div(per * place, BATCH), turns)
    pair, odd = lax.div(grp, 2), lax.rem(grp, 2)
    last_pair = groups // 2 - 1

    def when_owner(body):
        if everyone:
            body()
        else:
            pl.when(me < owners)(body)

    def greet_at(group, seq):
        pl.semaphore_signal(barrier, inc=1, device_id=(group, seq), device_id_type=MESH)

    barrier = pltpu.get_barrier_semaphore()
    greet_at(grp, mate)

    def greet(step, _):
        greet_at(grp, lax.rem(me + 2 * step, count))
        return 0

    lax.fori_loop(1, places, greet, 0)

    @pl.when(odd == 0)
    def _():
        greet_at(grp + 1, me)

    @pl.when(odd == 1)
    def _():
        greet_at(grp - 1, me)

    @pl.when(jnp.logical_and(odd == 0, pair > 0))
    def _():
        greet_at(grp - 1, me)

    @pl.when(jnp.logical_and(odd == 1, pair > 0))
    def _():
        greet_at(grp - 2, me)

    @pl.when(jnp.logical_and(odd == 1, pair < last_pair))
    def _():
        greet_at(grp + 1, me)
        greet_at(grp + 2, me)

    def turn_owners(turn, whose):
        start = far_first(jnp.int32(turn), own_turn, turns) * runs
        return [2 * (start + run) + whose for run in range(runs)]

    def owner_columns(owner):
        return pl.ds(pl.multiple_of(owner * (per * size), per * size), per * size)

    def load(owner):
        span = owner_columns(owner)
        return [
            pltpu.make_async_copy(far.at[:, span], near.at[:, span], load_sem.at[index, owner])
            for index, (far, near) in enumerate(
                [(d_hbm, d_ref), (k_hbm, k_ref), (v_hbm, v_ref)]
            )
        ]

    for turn in range(turns):
        for whose in (1 - side, side):
            for owner in turn_owners(turn, whose):
                for copy in load(owner):
                    copy.start()
    query_copy = pltpu.make_async_copy(q_hbm, q_ref, query_sem)
    query_copy.start()
    gate_copy = pltpu.make_async_copy(g_hbm, g_ref, gate_sem)
    gate_copy.start()

    beside = 1 + jnp.minimum(pair, 1) + 2 * odd * jnp.minimum(last_pair - pair, 1)
    pl.semaphore_wait(barrier, places + beside)

    def columns(head):
        return pl.ds(pl.multiple_of(head * size, size), size)

    def join(late, early):
        product = mul_wide(late[:, :size], early)
        return product[:, :size], product[:, size:] + late[:, size:]

    def apply(step, state):
        return mul(step[:, :size], state) + step[:, size:]

    def turn_spots(turn):
        return [
            lax.div(owner, 2) * per + index
            for owner in turn_owners(turn, side)
            for index in range(per)
        ]

    def compute(turn):
        turn_of = turn_owners(turn, 1 - side) + turn_owners(turn, side)
        for owner in turn_of:
            for copy in load(owner):
                copy.wait()
        picked = [owner * per + index for owner in turn_of for index in range(per)]
        spans = [columns(head) for head in picked]
        cums, shrunk, carry, steps = state_terms(
            [k_ref[:, span] for span in spans],
            [v_ref[:, span] for span in spans],
            [d_ref[:, span] for span in spans],
            [r_ref[pl.ds(head, 1), :] for head in picked],
        )
        for head, cum, shrink, carried in zip(picked, cums, shrunk, carry):
            kept_cum[head] = cum
            kept_key[head] = shrink
            kept_carry[head] = carried
        return steps

    def outputs(turn, whose):
        picked = [
            owner * per + index for owner in turn_owners(turn, whose) for index in range(per)
        ]
        results = output_terms(
            [q_ref[:, columns(head)] for head in picked],
            [kept_cum[head] for head in picked],
            [kept_key[head] for head in picked],
            [kept_carry[head] for head in picked],
            [r_ref[pl.ds(head, 1), :] for head in picked],
        )
        for head, (head_reach, head_local) in zip(picked, results):
            reach[head] = head_reach
            local[head] = head_local

    def mate_copy(spot, slot):
        return pltpu.make_async_remote_copy(
            src_ref=outgo.at[spot],
            dst_ref=duo.at[spot, slot],
            send_sem=mate_send.at[spot],
            recv_sem=mate_recv.at[spot],
            device_id=(grp, mate),
            device_id_type=MESH,
        )

    def up_copy(spot, shard, host):
        return pltpu.make_async_remote_copy(
            src_ref=comp.at[spot],
            dst_ref=arrived.at[shard, lax.rem(spot, per)],
            send_sem=up_send.at[spot],
            recv_sem=up_recv.at[shard, lax.rem(spot, per)],
            device_id=(grp, 2 * host + side),
            device_id_type=MESH,
        )

    def pair_up(turn):
        spots = turn_spots(turn)
        for spot in spots:
            mate_copy(spot, 1 - side).wait_recv()
        joined = [join(duo[spot, 1], duo[spot, 0]) for spot in spots]
        for spot, (whole, added) in zip(spots, joined):
            comp[spot, :, :size] = whole
            comp[spot, :, size:] = added
            host = lax.div(spot, per)

            @pl.when(host != place)
            def _():
                up_copy(spot, place, host).start()

            @pl.when(host == place)
            def _():
                arrived[place, lax.rem(spot, per)] = comp[spot]

    def first_phase(turn, _):
        spots = turn_spots(turn)
        steps = compute(turn)
        for spot, step in zip(spots, steps[:BATCH]):
            outgo[spot] = step
            mate_copy(spot, side).start()
        for spot, step in zip(spots, steps[BATCH:]):
            duo[spot, side] = step

        @pl.when(turn > 0)
        def _():
            pair_up(turn - 1)

        return 0

    lax.fori_loop(0, turns, first_phase, 0)
    pair_up(turns - 1)
    query_copy.wait()

    def mate_outputs(turn, _):
        outputs(turn, 1 - side)
        return 0

    lax.fori_loop(0, turns, mate_outputs, 0)

    rows = lax.broadcasted_iota(jnp.int32, (size, 2 * size), 0)
    cols = lax.broadcasted_iota(jnp.int32, (size, 2 * size), 1)

    def total_copy(target):
        return pltpu.make_async_remote_copy(
            src_ref=prior.at[places],
            dst_ref=total_in,
            send_sem=total_send,
            recv_sem=total_recv,
            device_id=(target, me),
            device_id_type=MESH,
        )

    def pair_copy(ahead):
        return pltpu.make_async_remote_copy(
            src_ref=onward,
            dst_ref=pair_in,
            send_sem=pair_send.at[ahead - 1],
            recv_sem=pair_recv,
            device_id=(grp + ahead, me),
            device_id_type=MESH,
        )

    def down_copy(shard, host):
        return pltpu.make_async_remote_copy(
            src_ref=starts.at[shard],
            dst_ref=slots.at[0, pl.ds(host * per, per)],
            send_sem=down_send.at[shard],
            recv_sem=down_recv.at[host],
            device_id=(grp, 2 * shard + side),
            device_id_type=MESH,
        )

    def relay_copy(host):
        return pltpu.make_async_remote_copy(
            src_ref=slots.at[1 - side, pl.ds(host * per, per)],
            dst_ref=begin.at[pl.ds(host * per, per)],
            send_sem=relay_send.at[host],
            recv_sem=relay_recv.at[host],
            device_id=(grp, mate),
            device_id_type=MESH,
        )

    def compose():
        for index in range(per):
            prior[0, index] = jnp.where(rows == cols, 1.0, 0.0).astype(F32)

        def advance(shard, _):
            @pl.when(shard != place)
            def _():
                for index in range(per):
                    up_copy(place * per + index, shard, place).wait_recv()

            for index in range(per):
                whole, added = join(arrived[shard, index], prior[shard, index])
                prior[shard + 1, index, :, :size] = whole
                prior[shard + 1, index, :, size:] = added
            return 0

        lax.fori_loop(0, places, advance, 0)

        @pl.when(odd == 0)
        def _():
            total_copy(grp + 1).start()

        @pl.when(pair == 0)
        def _():
            pair_in[...] = jnp.zeros_like(pair_in)

        @pl.when(odd == 1)
        def _():
            total_copy(grp).wait_recv()
            both = [join(prior[places, index], total_in[index]) for index in range(per)]

            @pl.when(pair > 0)
            def _():
                pair_copy(1).wait_recv()

            for index in range(per):
                onward[index] = mul(both[index][0], pair_in[index]) + both[index][1]

            @pl.when(pair < last_pair)
            def _():
                pair_copy(2).start()
                pair_copy(1).start()

            for index in range(per):
                entry[index] = apply(total_in[index], pair_in[index])

        @pl.when(odd == 0)
        def _():
            @pl.when(pair > 0)
            def _():
                pair_copy(1).wait_recv()

            entry[...] = pair_in[...]

        def give(step, _):
            shard = far_first(step, place, places)
            for index in range(per):
                starts[shard, index] = apply(prior[shard, index], entry[index])

            @pl.when(shard != place)
            def _():
                down_copy(shard, place).start()

            @pl.when(shard == place)
            def _():
                slots[0, pl.ds(place * per, per)] = starts[shard]

            return 0

        lax.fori_loop(0, places, give, 0)

    when_owner(compose)

    def own_outputs(turn, _):
        outputs(turn, side)
        return 0

    lax.fori_loop(0, turns, own_outputs, 0)
    gate_copy.wait()

    def finish(owner, states):
        for index in range(per):
            head = owner * per + index
            raw = mul(reach[head], states[index]) + local[head]
            scaled = raw * lax.rsqrt(jnp.mean(raw * raw, axis=-1, keepdims=True) + 1e-05)
            gate = g_ref[:, columns(head)].astype(F32)
            o_ref[:, columns(head)] = (scaled / (1.0 + jnp.exp(-gate))).astype(BF16)

    def nearest(step):
        return near_first(step, place, hosts) if everyone else step

    def relay(step, _):
        host = nearest(step)

        @pl.when(host != place)
        def _():
            down_copy(place, host).wait_recv()

        for index in range(per):
            spot = host * per + index
            slots[1, spot] = apply(duo[spot, 0], slots[0, spot])
        relay_copy(host).start()
        finish(2 * host + side, [slots[side, host * per + index] for index in range(per)])
        return 0

    lax.fori_loop(0, hosts, relay, 0)

    def last(step, _):
        host = nearest(step)
        relay_copy(host).wait_recv()
        finish(2 * host + 1 - side, [begin[host * per + index] for index in range(per)])
        return 0

    lax.fori_loop(0, hosts, last, 0)

    def drain(spot, _):
        mate_copy(spot, side).wait_send()
        host = lax.div(spot, per)

        @pl.when(host != place)
        def _():
            up_copy(spot, place, host).wait_send()

        return 0

    lax.fori_loop(0, heads // 2, drain, 0)

    def drain_down():
        @pl.when(odd == 0)
        def _():
            total_copy(grp + 1).wait_send()

        @pl.when(jnp.logical_and(odd == 1, pair < last_pair))
        def _():
            pair_copy(2).wait_send()
            pair_copy(1).wait_send()

        def one(shard, _):
            @pl.when(shard != place)
            def _():
                down_copy(shard, place).wait_send()

            return 0

        lax.fori_loop(0, places, one, 0)

    when_owner(drain_down)

    def drain_relay(host, _):
        relay_copy(host).wait_send()
        return 0

    lax.fori_loop(0, hosts, drain_relay, 0)


def shards(groups, count, queries, key_vectors, values, log_decay, write_rate, out_gate):
    seq_count, local_len, features = queries.shape
    heads = write_rate.shape[1]
    size = features // heads
    per = max(heads // count, 1)
    owners = heads // per
    half, places, hosts = heads // 2, count // 2, owners // 2
    dma = pltpu.SemaphoreType.DMA
    square = (size, size)
    wide = (size, 2 * size)
    call = pl.pallas_call(
        functools.partial(kernel, groups, count, heads),
        out_shape=jax.ShapeDtypeStruct((local_len, features), BF16),
        in_specs=[pl.BlockSpec(memory_space=pltpu.HBM)] * 5
        + [pl.BlockSpec(memory_space=pltpu.VMEM)],
        out_specs=pl.BlockSpec(memory_space=pltpu.VMEM),
        scratch_shapes=[pltpu.VMEM((local_len, features), BF16)] * 5
        + [
            pltpu.VMEM((half, *wide), F32),
            pltpu.VMEM((half, 2, *wide), F32),
            pltpu.VMEM((half, *wide), F32),
            pltpu.VMEM((places, per, *wide), F32),
            pltpu.VMEM((places + 1, per, *wide), F32),
            pltpu.VMEM((per, *wide), F32),
            pltpu.VMEM((per, *square), F32),
            pltpu.VMEM((per, *square), F32),
            pltpu.VMEM((per, *square), F32),
            pltpu.VMEM((places, per, *square), F32),
            pltpu.VMEM((2, half, *square), F32),
            pltpu.VMEM((half, *square), F32),
            pltpu.VMEM((heads, local_len, size), F32),
            pltpu.VMEM((heads, local_len, size), F32),
            pltpu.VMEM((heads, local_len, size), F32),
            pltpu.VMEM((heads, local_len, size), F32),
            pltpu.VMEM((heads, local_len, 2 * size), F32),
            dma((3, owners)),
            dma,
            dma,
            dma((half,)),
            dma((half,)),
            dma((half,)),
            dma((places, per)),
            dma,
            dma,
            dma((2,)),
            dma,
            dma((places,)),
            dma((hosts,)),
            dma((hosts,)),
            dma((hosts,)),
        ],
        compiler_params=pltpu.CompilerParams(
            collective_id=0, has_side_effects=True, vmem_limit_bytes=63 * 1024 * 1024
        ),
        name="delta_attention",
    )
    result = call(
        queries[0], key_vectors[0], values[0], log_decay[0], out_gate[0], write_rate[0]
    )
    return result[None]


def solution(mesh):
    spread = P(None, ("grp", "seq"), None)
    return jax.shard_map(
        functools.partial(shards, mesh.shape["grp"], mesh.shape["seq"]),
        mesh=mesh,
        in_specs=(spread, spread, spread, spread, P(None, None, ("grp", "seq")), spread),
        out_specs=spread,
        check_vma=False,
    )
```

```python
import functools
import jax
import jax.numpy as jnp
from jax import lax
from jax.experimental import pallas as pl
from jax.experimental.pallas import tpu as pltpu
from jax.sharding import PartitionSpec as P

BLOCK = 64
BATCH = 2
MESH = pl.DeviceIdType.MESH
F32 = jnp.float32
BF16 = jnp.bfloat16


def split(value):
    high = value.astype(BF16)
    return high, (value - high.astype(F32)).astype(BF16)


def mul(left, right):
    width = right.shape[1]
    lhs = jnp.concatenate(split(left), axis=1)
    parts = jnp.concatenate(split(right), axis=1)
    out = jnp.dot(lhs, jnp.concatenate([parts, parts], axis=0), preferred_element_type=F32)
    return out[:, :width] + out[:, width:]


def mul_split(left, right):
    width = right[0].shape[1]
    parts = jnp.concatenate(right, axis=1)
    out = jnp.dot(
        jnp.concatenate(left, axis=1),
        jnp.concatenate([parts, parts], axis=0),
        preferred_element_type=F32,
    )
    return out[:, :width] + out[:, width:]


def mul_rows(left, right):
    width = right.shape[0]
    lhs = jnp.concatenate(split(left), axis=1)
    parts = jnp.concatenate(split(right), axis=0)
    rhs = jnp.concatenate([parts, parts], axis=1)
    out = lax.dot_general(lhs, rhs, (((1,), (1,)), ((), ())), preferred_element_type=F32)
    return out[:, :width] + out[:, width:]


def mul_wide(left, right):
    high, low = split(left)
    r_high, r_low = split(right)
    lhs = jnp.concatenate([high, low], axis=1)
    rhs = jnp.concatenate([r_high, r_high], axis=0)
    return jnp.dot(lhs, rhs, preferred_element_type=F32) + jnp.dot(
        high, r_low, preferred_element_type=F32
    )


def mul_both(upper, lower, right):
    width = right[0].shape[1]
    lhs = jnp.concatenate(
        [jnp.concatenate([up, low], axis=0) for up, low in zip(upper, lower)], axis=1
    )
    parts = jnp.concatenate(right, axis=1)
    out = jnp.dot(lhs, jnp.concatenate([parts, parts], axis=0), preferred_element_type=F32)
    return out[:, :width] + out[:, width:]


def state_terms(keys, values, decays, rates):
    extent, size = keys[0].shape
    half = extent // 2
    rows = lax.broadcasted_iota(jnp.int32, (extent, extent), 0)
    cols = lax.broadcasted_iota(jnp.int32, (extent, extent), 1)
    same = (rows >= half) == (cols >= half)
    eye = jnp.where(rows == cols, 1.0, 0.0).astype(F32)
    ones = jnp.where(rows >= cols, 1.0, 0.0).astype(BF16)
    cums = [jnp.dot(ones, decay, preferred_element_type=F32) for decay in decays]
    units = []
    for key in keys:
        key_f = key.astype(F32)
        units.append(key_f * lax.rsqrt(jnp.sum(key_f * key_f, axis=-1, keepdims=True) + 1e-06))
    shrunk = [unit * jnp.exp(cum[half - 1 : half] - cum) for unit, cum in zip(units, cums)]
    pairs = [
        mul_rows(unit * jnp.exp(cum - cum[half - 1 : half]), shrink)
        for unit, cum, shrink in zip(units, cums, shrunk)
    ]
    lowers = [jnp.where(rows > cols, product * rate, 0.0) for product, rate in zip(pairs, rates)]
    diag = [jnp.where(same, lower, 0.0) for lower in lowers]
    below = [jnp.where(same, 0.0, lower) for lower in lowers]
    inverse = [eye - part for part in diag]
    power = [split(mul(part, part)) for part in diag]
    for _ in range(half.bit_length() - 3):
        both = [mul_both(split(x), p, p) for x, p in zip(inverse, power)]
        inverse = [x + b[:extent] for x, b in zip(inverse, both)]
        power = [split(b[extent:]) for b in both]
    inverse = [x + mul_split(split(x), p) for x, p in zip(inverse, power)]
    corner = [mul(x[half:], c) for x, c in zip(inverse, below)]
    corner = [mul(c, x) for c, x in zip(corner, inverse)]
    inverse = [
        jnp.concatenate([x[:half], x[half:] - c], axis=0) for x, c in zip(inverse, corner)
    ]
    carry = [
        mul_wide(x, jnp.concatenate([unit * jnp.exp(cum), value.astype(F32)], axis=1))
        for x, unit, cum, value in zip(inverse, units, cums, values)
    ]
    steps = []
    for unit, cum, rate, carried in zip(units, cums, rates, carry):
        last = cum[extent - 1 : extent]
        key_end = jnp.transpose(unit * jnp.exp(last - cum)) * rate
        out = mul_wide(key_end, carried)
        step_map = jnp.where(rows == cols, jnp.exp(last), 0.0) - out[:, :size]
        steps.append(jnp.concatenate([step_map, out[:, size:]], axis=1))
    return cums, shrunk, carry, steps


def output_terms(queries, cums, shrunk, carry, rates):
    extent, size = queries[0].shape
    half = extent // 2
    rows = lax.broadcasted_iota(jnp.int32, (extent, extent), 0)
    cols = lax.broadcasted_iota(jnp.int32, (extent, extent), 1)
    q_f = [query.astype(F32) for query in queries]
    pairs = [
        mul_rows(query * jnp.exp(cum - cum[half - 1 : half]), shrink)
        for query, cum, shrink in zip(q_f, cums, shrunk)
    ]
    attends = [jnp.where(rows >= cols, product * rate, 0.0) for product, rate in zip(pairs, rates)]
    outs = [mul_wide(attend, carried) for attend, carried in zip(attends, carry)]
    return [
        (query * jnp.exp(cum) - out[:, :size], out[:, size:])
        for query, cum, out in zip(q_f, cums, outs)
    ]


def flip(own, high, low):
    return 2 * lax.rem(lax.div(own, 2) + high, 2) + lax.rem(lax.rem(own, 2) + low, 2)


def far_first(step, own, extent):
    if extent != 4:
        return lax.rem(own + 1 + step, extent)
    late = lax.div(step, 2)
    return flip(own, 1 - late, lax.rem(step + late, 2))


def near_first(step, own, extent):
    if extent != 4:
        return lax.rem(own + extent - step, extent)
    return flip(own, lax.div(step, 2), lax.rem(step, 2))


def kernel(
    groups, count, heads,
    q_hbm, k_hbm, v_hbm, d_hbm, g_hbm, r_ref, o_ref,
    q_ref, k_ref, v_ref, d_ref, g_ref,
    outgo, duo, comp, arrived, prior, total_in, pair_in, entry, onward, starts, slots, begin,
    reach, local, kept_cum, kept_key, kept_carry,
    load_sem, query_sem, gate_sem, mate_send, mate_recv, up_send, up_recv,
    total_send, total_recv, pair_send, pair_recv, down_send, down_recv, relay_send, relay_recv,
):
    grp, me = lax.axis_index("grp"), lax.axis_index("seq")
    per = max(heads // count, 1)
    owners = heads // per
    size = q_ref.shape[1] // heads
    everyone = owners == count
    places, hosts = count // 2, owners // 2
    place, side = lax.div(me, 2), lax.rem(me, 2)
    mate = me + 1 - 2 * side
    turns = heads // 2 // BATCH
    runs = BATCH // per
    own_turn = lax.rem(lax.div(per * place, BATCH), turns)
    pair, odd = lax.div(grp, 2), lax.rem(grp, 2)
    last_pair = groups // 2 - 1

    def when_owner(body):
        if everyone:
            body()
        else:
            pl.when(me < owners)(body)

    def greet_at(group, seq):
        pl.semaphore_signal(barrier, inc=1, device_id=(group, seq), device_id_type=MESH)

    barrier = pltpu.get_barrier_semaphore()
    greet_at(grp, mate)

    def greet(step, _):
        greet_at(grp, lax.rem(me + 2 * step, count))
        return 0

    lax.fori_loop(1, places, greet, 0)

    @pl.when(odd == 0)
    def _():
        greet_at(grp + 1, me)

    @pl.when(odd == 1)
    def _():
        greet_at(grp - 1, me)

    @pl.when(jnp.logical_and(odd == 0, pair > 0))
    def _():
        greet_at(grp - 1, me)

    @pl.when(jnp.logical_and(odd == 1, pair > 0))
    def _():
        greet_at(grp - 2, me)

    @pl.when(jnp.logical_and(odd == 1, pair < last_pair))
    def _():
        greet_at(grp + 1, me)
        greet_at(grp + 2, me)

    def turn_owners(turn, whose):
        start = far_first(jnp.int32(turn), own_turn, turns) * runs
        return [2 * (start + run) + whose for run in range(runs)]

    def owner_columns(owner):
        return pl.ds(pl.multiple_of(owner * (per * size), per * size), per * size)

    def load(owner):
        span = owner_columns(owner)
        return [
            pltpu.make_async_copy(far.at[:, span], near.at[:, span], load_sem.at[index, owner])
            for index, (far, near) in enumerate(
                [(d_hbm, d_ref), (k_hbm, k_ref), (v_hbm, v_ref)]
            )
        ]

    for turn in range(turns):
        for whose in (1 - side, side):
            for owner in turn_owners(turn, whose):
                for copy in load(owner):
                    copy.start()
    query_copy = pltpu.make_async_copy(q_hbm, q_ref, query_sem)
    query_copy.start()
    gate_copy = pltpu.make_async_copy(g_hbm, g_ref, gate_sem)
    gate_copy.start()

    beside = 1 + jnp.minimum(pair, 1) + 2 * odd * jnp.minimum(last_pair - pair, 1)
    pl.semaphore_wait(barrier, places + beside)

    def columns(head):
        return pl.ds(pl.multiple_of(head * size, size), size)

    def join(late, early):
        product = mul_wide(late[:, :size], early)
        return product[:, :size], product[:, size:] + late[:, size:]

    def apply(step, state):
        return mul(step[:, :size], state) + step[:, size:]

    def turn_spots(turn):
        return [
            lax.div(owner, 2) * per + index
            for owner in turn_owners(turn, side)
            for index in range(per)
        ]

    def compute(turn):
        turn_of = turn_owners(turn, 1 - side) + turn_owners(turn, side)
        for owner in turn_of:
            for copy in load(owner):
                copy.wait()
        picked = [owner * per + index for owner in turn_of for index in range(per)]
        spans = [columns(head) for head in picked]
        cums, shrunk, carry, steps = state_terms(
            [k_ref[:, span] for span in spans],
            [v_ref[:, span] for span in spans],
            [d_ref[:, span] for span in spans],
            [r_ref[pl.ds(head, 1), :] for head in picked],
        )
        for head, cum, shrink, carried in zip(picked, cums, shrunk, carry):
            kept_cum[head] = cum
            kept_key[head] = shrink
            kept_carry[head] = carried
        return steps

    def outputs(turn, whose):
        picked = [
            owner * per + index for owner in turn_owners(turn, whose) for index in range(per)
        ]
        results = output_terms(
            [q_ref[:, columns(head)] for head in picked],
            [kept_cum[head] for head in picked],
            [kept_key[head] for head in picked],
            [kept_carry[head] for head in picked],
            [r_ref[pl.ds(head, 1), :] for head in picked],
        )
        for head, (head_reach, head_local) in zip(picked, results):
            reach[head] = head_reach
            local[head] = head_local

    def mate_copy(spot, slot):
        return pltpu.make_async_remote_copy(
            src_ref=outgo.at[spot],
            dst_ref=duo.at[spot, slot],
            send_sem=mate_send.at[spot],
            recv_sem=mate_recv.at[spot],
            device_id=(grp, mate),
            device_id_type=MESH,
        )

    def up_copy(spot, shard, host):
        return pltpu.make_async_remote_copy(
            src_ref=comp.at[spot],
            dst_ref=arrived.at[shard, lax.rem(spot, per)],
            send_sem=up_send.at[spot],
            recv_sem=up_recv.at[shard, lax.rem(spot, per)],
            device_id=(grp, 2 * host + side),
            device_id_type=MESH,
        )

    def pair_up(turn):
        spots = turn_spots(turn)
        for spot in spots:
            mate_copy(spot, 1 - side).wait_recv()
        joined = [join(duo[spot, 1], duo[spot, 0]) for spot in spots]
        for spot, (whole, added) in zip(spots, joined):
            comp[spot, :, :size] = whole
            comp[spot, :, size:] = added
            host = lax.div(spot, per)

            @pl.when(host != place)
            def _():
                up_copy(spot, place, host).start()

            @pl.when(host == place)
            def _():
                arrived[place, lax.rem(spot, per)] = comp[spot]

    def first_phase(turn, _):
        spots = turn_spots(turn)
        steps = compute(turn)
        for spot, step in zip(spots, steps[:BATCH]):
            outgo[spot] = step
            mate_copy(spot, side).start()
        for spot, step in zip(spots, steps[BATCH:]):
            duo[spot, side] = step

        @pl.when(turn > 0)
        def _():
            pair_up(turn - 1)

        return 0

    lax.fori_loop(0, turns, first_phase, 0)
    pair_up(turns - 1)
    query_copy.wait()

    rows = lax.broadcasted_iota(jnp.int32, (size, 2 * size), 0)
    cols = lax.broadcasted_iota(jnp.int32, (size, 2 * size), 1)

    def total_copy(target):
        return pltpu.make_async_remote_copy(
            src_ref=prior.at[places],
            dst_ref=total_in,
            send_sem=total_send,
            recv_sem=total_recv,
            device_id=(target, me),
            device_id_type=MESH,
        )

    def pair_copy(ahead):
        return pltpu.make_async_remote_copy(
            src_ref=onward,
            dst_ref=pair_in,
            send_sem=pair_send.at[ahead - 1],
            recv_sem=pair_recv,
            device_id=(grp + ahead, me),
            device_id_type=MESH,
        )

    def down_copy(shard, host):
        return pltpu.make_async_remote_copy(
            src_ref=starts.at[shard],
            dst_ref=slots.at[0, pl.ds(host * per, per)],
            send_sem=down_send.at[shard],
            recv_sem=down_recv.at[host],
            device_id=(grp, 2 * shard + side),
            device_id_type=MESH,
        )

    def relay_copy(host):
        return pltpu.make_async_remote_copy(
            src_ref=slots.at[1 - side, pl.ds(host * per, per)],
            dst_ref=begin.at[pl.ds(host * per, per)],
            send_sem=relay_send.at[host],
            recv_sem=relay_recv.at[host],
            device_id=(grp, mate),
            device_id_type=MESH,
        )

    def compose():
        for index in range(per):
            prior[0, index] = jnp.where(rows == cols, 1.0, 0.0).astype(F32)

        def advance(shard, _):
            @pl.when(shard != place)
            def _():
                for index in range(per):
                    up_copy(place * per + index, shard, place).wait_recv()

            for index in range(per):
                whole, added = join(arrived[shard, index], prior[shard, index])
                prior[shard + 1, index, :, :size] = whole
                prior[shard + 1, index, :, size:] = added
            return 0

        lax.fori_loop(0, places, advance, 0)

        @pl.when(odd == 0)
        def _():
            total_copy(grp + 1).start()

        @pl.when(pair == 0)
        def _():
            pair_in[...] = jnp.zeros_like(pair_in)

        @pl.when(odd == 1)
        def _():
            total_copy(grp).wait_recv()
            both = [join(prior[places, index], total_in[index]) for index in range(per)]

            @pl.when(pair > 0)
            def _():
                pair_copy(1).wait_recv()

            for index in range(per):
                onward[index] = mul(both[index][0], pair_in[index]) + both[index][1]

            @pl.when(pair < last_pair)
            def _():
                pair_copy(2).start()
                pair_copy(1).start()

            for index in range(per):
                entry[index] = apply(total_in[index], pair_in[index])

        @pl.when(odd == 0)
        def _():
            @pl.when(pair > 0)
            def _():
                pair_copy(1).wait_recv()

            entry[...] = pair_in[...]

        def give(step, _):
            shard = far_first(step, place, places)
            for index in range(per):
                starts[shard, index] = apply(prior[shard, index], entry[index])

            @pl.when(shard != place)
            def _():
                down_copy(shard, place).start()

            @pl.when(shard == place)
            def _():
                slots[0, pl.ds(place * per, per)] = starts[shard]

            return 0

        lax.fori_loop(0, places, give, 0)

    def own_outputs(turn, _):
        outputs(turn, side)
        return 0

    lax.fori_loop(0, turns, own_outputs, 0)
    when_owner(compose)

    gate_copy.wait()

    def finish(owner, states):
        for index in range(per):
            head = owner * per + index
            raw = mul(reach[head], states[index]) + local[head]
            scaled = raw * lax.rsqrt(jnp.mean(raw * raw, axis=-1, keepdims=True) + 1e-05)
            gate = g_ref[:, columns(head)].astype(F32)
            o_ref[:, columns(head)] = (scaled / (1.0 + jnp.exp(-gate))).astype(BF16)

    def nearest(step):
        return near_first(step, place, hosts) if everyone else step

    def relay(step, _):
        host = nearest(step)

        @pl.when(step < turns)
        def _():
            outputs(step, 1 - side)

        @pl.when(host != place)
        def _():
            down_copy(place, host).wait_recv()

        for index in range(per):
            spot = host * per + index
            slots[1, spot] = apply(duo[spot, 0], slots[0, spot])
        relay_copy(host).start()
        finish(2 * host + side, [slots[side, host * per + index] for index in range(per)])
        return 0

    lax.fori_loop(0, hosts, relay, 0)

    def last(step, _):
        host = nearest(step)
        relay_copy(host).wait_recv()
        finish(2 * host + 1 - side, [begin[host * per + index] for index in range(per)])
        return 0

    lax.fori_loop(0, hosts, last, 0)

    def drain(spot, _):
        mate_copy(spot, side).wait_send()
        host = lax.div(spot, per)

        @pl.when(host != place)
        def _():
            up_copy(spot, place, host).wait_send()

        return 0

    lax.fori_loop(0, heads // 2, drain, 0)

    def drain_down():
        @pl.when(odd == 0)
        def _():
            total_copy(grp + 1).wait_send()

        @pl.when(jnp.logical_and(odd == 1, pair < last_pair))
        def _():
            pair_copy(2).wait_send()
            pair_copy(1).wait_send()

        def one(shard, _):
            @pl.when(shard != place)
            def _():
                down_copy(shard, place).wait_send()

            return 0

        lax.fori_loop(0, places, one, 0)

    when_owner(drain_down)

    def drain_relay(host, _):
        relay_copy(host).wait_send()
        return 0

    lax.fori_loop(0, hosts, drain_relay, 0)


def shards(groups, count, queries, key_vectors, values, log_decay, write_rate, out_gate):
    seq_count, local_len, features = queries.shape
    heads = write_rate.shape[1]
    size = features // heads
    per = max(heads // count, 1)
    owners = heads // per
    half, places, hosts = heads // 2, count // 2, owners // 2
    dma = pltpu.SemaphoreType.DMA
    square = (size, size)
    wide = (size, 2 * size)
    call = pl.pallas_call(
        functools.partial(kernel, groups, count, heads),
        out_shape=jax.ShapeDtypeStruct((local_len, features), BF16),
        in_specs=[pl.BlockSpec(memory_space=pltpu.HBM)] * 5
        + [pl.BlockSpec(memory_space=pltpu.VMEM)],
        out_specs=pl.BlockSpec(memory_space=pltpu.VMEM),
        scratch_shapes=[pltpu.VMEM((local_len, features), BF16)] * 5
        + [
            pltpu.VMEM((half, *wide), F32),
            pltpu.VMEM((half, 2, *wide), F32),
            pltpu.VMEM((half, *wide), F32),
            pltpu.VMEM((places, per, *wide), F32),
            pltpu.VMEM((places + 1, per, *wide), F32),
            pltpu.VMEM((per, *wide), F32),
            pltpu.VMEM((per, *square), F32),
            pltpu.VMEM((per, *square), F32),
            pltpu.VMEM((per, *square), F32),
            pltpu.VMEM((places, per, *square), F32),
            pltpu.VMEM((2, half, *square), F32),
            pltpu.VMEM((half, *square), F32),
            pltpu.VMEM((heads, local_len, size), F32),
            pltpu.VMEM((heads, local_len, size), F32),
            pltpu.VMEM((heads, local_len, size), F32),
            pltpu.VMEM((heads, local_len, size), F32),
            pltpu.VMEM((heads, local_len, 2 * size), F32),
            dma((3, owners)),
            dma,
            dma,
            dma((half,)),
            dma((half,)),
            dma((half,)),
            dma((places, per)),
            dma,
            dma,
            dma((2,)),
            dma,
            dma((places,)),
            dma((hosts,)),
            dma((hosts,)),
            dma((hosts,)),
        ],
        compiler_params=pltpu.CompilerParams(
            collective_id=0, has_side_effects=True, vmem_limit_bytes=63 * 1024 * 1024
        ),
        name="delta_attention",
    )
    result = call(
        queries[0], key_vectors[0], values[0], log_decay[0], out_gate[0], write_rate[0]
    )
    return result[None]


def solution(mesh):
    spread = P(None, ("grp", "seq"), None)
    return jax.shard_map(
        functools.partial(shards, mesh.shape["grp"], mesh.shape["seq"]),
        mesh=mesh,
        in_specs=(spread, spread, spread, spread, P(None, None, ("grp", "seq")), spread),
        out_specs=spread,
        check_vma=False,
    )
```
